256 devices in a mesh: shard: 64 (over y, z, core), group: 4 (over x).
Axes of the slice: x: 4, y: 4, z: 8, core: 2. Of those that a mesh axis runs over, the one named last changes fastest.
Arguments:
- embeddings: bfloat16 [1024, 512, 768], P(('shard', 'group')), may hold values from -50 to 50, as said below
- partners: int32 [1024, 8], P(('shard', 'group')), may hold values from -1 to 1023, as said below
- cluster: int32 [1024], P(('shard', 'group')), may hold values from 0 to 255, never falling along the last dimension, each value on 1 to 8 neighbouring positions
- counts: int32 [1024], P(('shard', 'group')), may hold values from 128 to 512
Outputs:
- maxsim: float32 [1024, 512], P(('shard', 'group'))
The draws below stay inside these ranges and needn't reach their ends.
Inputs may be any that keep to these rules, and one draw needn't show every extreme that they name: `partners`: entry k of block a's list is a + k or -1; entry 0 is always a itself; no entry passes the last block. Never falling along the blocks; each cluster spans 1 to 8 consecutive blocks. Real-valued embeddings of no particular norm.
All inputs are finite; a program needn't handle non-finite values.
Results may differ from the reference program's by a relative error of at most 0.0007.
Values may be sent and summed in bfloat16 or wider, within the bound.
A program may use at most 64 MiB of HBM per device.

```python
import math
import jax
import jax.numpy as jnp
import numpy as np
from jax import lax

W = 768
ROWS = 512
MAXC = 8
NBLK = 1024
CLUSTERS = 256


def draw_embeddings(key, part):
    key = jax.random.fold_in(key, 11)
    noise_key = jax.random.fold_in(key, 1)
    block_key = jax.random.fold_in(key, 2)
    row_key = jax.random.fold_in(key, 3)
    weight_key = jax.random.fold_in(key, 4)
    noise_field = jax.random.truncated_normal(noise_key, -4.0, 4.0, (NBLK, ROWS, W), jnp.float32)
    block_step = jax.random.randint(block_key, (NBLK, ROWS), 0, MAXC)
    source_block = ((jnp.arange(NBLK, dtype=jnp.int32)[:, None] + block_step) % NBLK).astype(jnp.int32)
    source_row = jax.random.randint(row_key, (NBLK, ROWS), 0, ROWS).astype(jnp.int32)
    strength = jax.random.uniform(weight_key, (NBLK, ROWS, 1), jnp.float32, 0.3, 1.2)
    copied = noise_field[source_block, source_row]
    blended = noise_field + strength * copied
    return blended.astype(jnp.bfloat16)


def draw_partners(key, part):
    key = jax.random.fold_in(key, 23)
    chosen = jax.random.randint(key, (NBLK, MAXC), 0, 5) < 3
    slot_ids = jnp.arange(MAXC, dtype=jnp.int32)
    candidate = jnp.arange(NBLK, dtype=jnp.int32)[:, None] + slot_ids[None, :]
    chosen = chosen | (slot_ids[None, :] == 0)
    return jnp.where(chosen & (candidate < NBLK), candidate, -1).astype(jnp.int32)


def place_ends(drawn, own_key, least, largest):
    shape = drawn.shape
    spot = [jax.random.randint(jax.random.fold_in(own_key, axis), (), 0, shape[axis]) for axis in range(len(shape))]
    drawn = drawn.at[tuple(spot)].set(least)
    longest = shape.index(max(shape))
    spot[longest] = (spot[longest] + 1) % shape[longest]
    return drawn.at[tuple(spot)].set(largest)


def profile(number_of, total, most, lean):
    portions = [(1 << 20) // math.isqrt(grade ** lean) + 1 for grade in range(2, number_of + 1)]
    rest, given = total - most - (number_of - 1), [1] * (number_of - 1)
    while rest > 0:
        candidates = [i for i in range(number_of - 1) if given[i] < most]
        whole, budget = sum([portions[i] for i in candidates]), rest
        for i in candidates:
            extra = min(most - given[i], max(1, budget * portions[i] // whole), rest)
            given[i] = given[i] + extra
            rest = rest - extra
    return np.array([most] + given)


def ragged_sizes(stream_key, count, total, bound, lean):
    if count == 2:
        one = jax.random.randint(stream_key, (), max(1, total - bound), min(bound, total - 1) + 1)
        return jnp.stack([one, total - one])
    sizes = jnp.asarray(profile(count, total, bound, lean), jnp.int32)
    pairs = (count - 1) // 2
    donor, sink = sizes[1:1 + 2 * pairs:2], sizes[2:2 + 2 * pairs:2]
    slack = jnp.minimum(donor - 1, bound - sink)
    moved = jax.random.randint(jax.random.fold_in(stream_key, 1), (pairs,), 0, 1 << 20) % (slack + 1)
    sizes = sizes.at[1:1 + 2 * pairs:2].set(donor - moved).at[2:2 + 2 * pairs:2].set(sink + moved)
    return sizes[jax.random.permutation(jax.random.fold_in(stream_key, 2), count)]


def setup_inputs(seed: int = 0) -> dict:
    streams_of = jax.random.split(jax.random.key(seed), 5)
    embeddings = draw_embeddings(jax.random.fold_in(streams_of[4], 71), 0)
    partners = draw_partners(jax.random.fold_in(streams_of[4], 71), 0)
    cluster = jnp.searchsorted(jnp.cumsum(ragged_sizes(streams_of[2], CLUSTERS, NBLK, MAXC, 2)), jnp.arange(NBLK), side="right").astype(jnp.int32)
    counts = place_ends(jax.random.randint(streams_of[3], (NBLK,), ROWS // 4, ROWS + 1), jax.random.fold_in(streams_of[3], 1), ROWS // 4, ROWS).astype(jnp.int32)
    return {"embeddings": embeddings, "partners": partners, "cluster": cluster, "counts": counts}


def reference(embeddings, partners, cluster, counts):
    floats = embeddings.astype(jnp.float32)
    unit_rows = (floats * lax.rsqrt(lax.optimization_barrier(jnp.sum(floats * floats, axis=-1, keepdims=True)) + 1e-06)).astype(jnp.bfloat16)
    slots = partners.shape[1]
    row_ids = jnp.arange(ROWS, dtype=jnp.int32)
    flat_list = partners.reshape(-1)

    def advance(best_sim, pair_index):
        first_block = (pair_index // slots).astype(jnp.int32)
        partner = flat_list[pair_index]
        partner_safe = jnp.maximum(partner, 0).astype(jnp.int32)
        active = (partner >= 0) & (cluster[partner_safe] == cluster[first_block])

        def update(running):
            left_unit = lax.dynamic_index_in_dim(unit_rows, first_block, 0, keepdims=False)
            right_unit = lax.dynamic_index_in_dim(unit_rows, partner_safe, 0, keepdims=False)
            scores = jnp.dot(left_unit, right_unit.T, preferred_element_type=jnp.float32)
            allowed = (row_ids[:, None] < counts[first_block]) & (row_ids[None, :] < counts[partner_safe])
            allowed = allowed & jnp.logical_not((partner_safe == first_block) & (row_ids[:, None] == row_ids[None, :]))
            scores = jnp.where(allowed, scores, jnp.float32(-2.0))
            running = running.at[first_block].max(lax.optimization_barrier(jnp.max(scores, axis=1)))
            running = running.at[partner_safe].max(lax.optimization_barrier(jnp.max(scores, axis=0)))
            return running

        def unchanged(running):
            return running
        return (lax.cond(active, update, unchanged, best_sim), None)
    start_sim = jnp.full((partners.shape[0], ROWS), -1.0, jnp.float32)
    best_sim, _ = lax.scan(advance, start_sim, jnp.arange(flat_list.shape[0], dtype=jnp.int32))
    return jnp.where(row_ids[None, :] < counts[:, None], best_sim, jnp.float32(0.0))
```

```python
import functools

import jax
import jax.numpy as jnp
from jax import lax
from jax.experimental import pallas as pl
from jax.experimental.pallas import tpu as pltpu
from jax.sharding import PartitionSpec as P

MESH = pl.DeviceIdType.MESH
AXES = ("shard", "group")
CHUNK = 256
PER = 4
SIDE = 8
LOW = -4.0


def scored(slot, rows, partner, window):
    return lax.dot_general(
        window[slot, rows, :],
        window[partner],
        (((1,), (1,)), ((), ())),
        preferred_element_type=jnp.float32,
    )


def fold_rows(scores):
    rows, columns = scores.shape
    return jnp.max(scores.reshape(rows // 8, 8, columns), axis=0)


def fold_columns(scores):
    best = scores[:, 0:128]
    for start in range(128, scores.shape[1], 128):
        best = jnp.maximum(best, scores[:, start : start + 128])
    return best


def kernel(
    devices,
    emb,
    partners,
    cluster,
    counts,
    out,
    window,
    info,
    facts,
    col_best,
    row_part,
    row_best,
    sent_best,
    got_best,
    load_sem,
    emb_send,
    emb_recv,
    info_send,
    info_recv,
    facts_sem,
    best_send,
    best_recv,
):
    rows_all = window.shape[1]
    chunks = rows_all // CHUNK
    shards = lax.axis_size("shard")
    groups = lax.axis_size("group")
    me = lax.axis_index("shard") * groups + lax.axis_index("group")
    total = shards * groups

    def place(index):
        index = lax.rem(index + total, total)
        return (lax.div(index, groups), lax.rem(index, groups))

    right, left = place(me + 1), place(me - 1)

    def leftwards(index):
        return lax.rem(lax.div(index + total, groups), 2) == 0

    right_meets_here = leftwards(me)
    left_meets_here = jnp.logical_not(leftwards(me + total - 1))

    barrier = pltpu.get_barrier_semaphore()
    for neighbour in (left, right):
        pl.semaphore_signal(barrier, inc=1, device_id=neighbour, device_id_type=MESH)

    def load_own(block):
        return pltpu.make_async_copy(emb.at[block], window.at[PER + block], load_sem.at[block])

    for block in range(PER):
        load_own(block).start()

    info[1] = jnp.zeros(info.shape[1:], jnp.int32)
    info[1, 0:PER, 0:SIDE] = partners[...]
    for block in range(PER):
        info[1, PER + block : PER + block + 1, :] = jnp.full((1, 128), cluster[block], jnp.int32)
        info[1, 2 * PER + block : 2 * PER + block + 1, :] = jnp.full((1, 128), counts[block], jnp.int32)
    pl.semaphore_wait(barrier, 2)

    info_left = pltpu.make_async_remote_copy(
        src_ref=info.at[1], dst_ref=info.at[2], send_sem=info_send.at[0], recv_sem=info_recv.at[0],
        device_id=left, device_id_type=MESH,
    )
    info_right = pltpu.make_async_remote_copy(
        src_ref=info.at[1], dst_ref=info.at[0], send_sem=info_send.at[1], recv_sem=info_recv.at[1],
        device_id=right, device_id_type=MESH,
    )
    info_left.start()
    info_right.start()

    def push(step, chunk, leftward):
        block = step if leftward else PER - 1 - step
        slot = 2 * PER + step if leftward else PER - 1 - step
        rows = pl.ds(chunk * CHUNK, CHUNK)
        side = 0 if leftward else 1
        return pltpu.make_async_remote_copy(
            src_ref=emb.at[block, rows, :],
            dst_ref=window.at[slot, rows, :],
            send_sem=emb_send.at[side, step, chunk],
            recv_sem=emb_recv.at[side, step, chunk],
            device_id=left if leftward else right,
            device_id_type=MESH,
        )

    sends_last_left = jnp.logical_not(left_meets_here)
    sends_last_right = jnp.logical_not(right_meets_here)
    for step in range(PER - 1):
        for chunk in range(chunks):
            push(step, chunk, True).start()
            push(step, chunk, False).start()

    @pl.when(sends_last_left)
    def _():
        for chunk in range(chunks):
            push(PER - 1, chunk, True).start()

    @pl.when(sends_last_right)
    def _():
        for chunk in range(chunks):
            push(PER - 1, chunk, False).start()

    col_best[...] = jnp.full(col_best.shape, LOW, jnp.float32)
    row_best[...] = jnp.full(row_best.shape, LOW, jnp.float32)
    for block in range(PER):
        load_own(block).wait()
    info_left.wait()
    info_right.wait()
    to_facts = pltpu.make_async_copy(info, facts, facts_sem)
    to_facts.start()
    to_facts.wait()

    def count_of(slot):
        return facts[lax.div(slot, PER), 2 * PER + lax.rem(slot, PER), 0]

    def penalty(slot, other):
        first, second = jnp.minimum(slot, other), jnp.maximum(slot, other)
        device_a, block_a = lax.div(first, PER), lax.rem(first, PER)
        device_b, block_b = lax.div(second, PER), lax.rem(second, PER)
        listed = facts[device_a, block_a, second - first] >= 0
        same = facts[device_a, PER + block_a, 0] == facts[device_b, PER + block_b, 0]
        return jnp.where(listed & same, jnp.float32(0.0), jnp.float32(LOW))

    def normalise(slot, chunk):
        rows = pl.ds(pl.multiple_of(chunk * CHUNK, CHUNK), CHUNK)
        floats = window[slot, rows, :].astype(jnp.float32)
        unit = floats * lax.rsqrt(jnp.sum(floats * floats, axis=-1, keepdims=True) + 1e-06)
        head = window[slot, 0:16, :].astype(jnp.float32)[0:1, :]
        head = jnp.where(chunk == 0, unit[0:1, :], head)
        ids = chunk * CHUNK + lax.broadcasted_iota(jnp.int32, (CHUNK, 1), 0)
        window[slot, rows, :] = jnp.where(ids < count_of(slot), unit, head).astype(jnp.bfloat16)

    def meet(slot, chunk, low, high):
        rows = pl.ds(pl.multiple_of(chunk * CHUNK, CHUNK), CHUNK)
        row_part[...] = jnp.full(row_part.shape, LOW, jnp.float32)

        def one(other, carry):
            scores = scored(slot, rows, other, window)
            cost = penalty(slot, other)
            col_best[other] = jnp.maximum(col_best[other], fold_rows(scores) + cost)
            row_part[...] = jnp.maximum(row_part[...], fold_columns(scores) + cost)
            return carry

        lax.fori_loop(low, high, one, 0)
        best = jnp.max(row_part[...].T, axis=0, keepdims=True)
        row_best[slot, :, rows] = jnp.broadcast_to(best, (8, CHUNK))

    def own_normalise(index, carry):
        normalise(PER + lax.div(index, chunks), lax.rem(index, chunks))
        return carry

    lax.fori_loop(0, PER * chunks, own_normalise, 0)

    def own_step(index, carry):
        slot, chunk = PER + lax.div(index, chunks), lax.rem(index, chunks)
        meet(slot, chunk, PER, slot)
        rows = pl.ds(pl.multiple_of(chunk * CHUNK, CHUNK), CHUNK)
        scores = scored(slot, rows, slot, window)
        row_ids = chunk * CHUNK + lax.broadcasted_iota(jnp.int32, scores.shape, 0)
        col_ids = lax.broadcasted_iota(jnp.int32, scores.shape, 1)
        allowed = (row_ids < count_of(slot)) & (row_ids != col_ids)
        scores = jnp.where(allowed, scores, jnp.float32(LOW))
        col_best[slot] = jnp.maximum(col_best[slot], fold_rows(scores) + penalty(slot, slot))
        return carry

    lax.fori_loop(0, PER * chunks, own_step, 0)

    def arrived(step, chunk, side, slot):
        rows = pl.ds(pl.multiple_of(chunk * CHUNK, CHUNK), CHUNK)
        return pltpu.make_async_remote_copy(
            src_ref=emb.at[0, rows, :],
            dst_ref=window.at[slot, rows, :],
            send_sem=emb_send.at[side, step, chunk],
            recv_sem=emb_recv.at[side, step, chunk],
            device_id=left,
            device_id_type=MESH,
        )

    def exchange_step(index, carry):
        step, side = lax.div(index, 2), lax.rem(index, 2)
        from_right = side == 0
        slot = jnp.where(from_right, 2 * PER + step, PER - 1 - step)
        with_own = jnp.where(from_right, right_meets_here, left_meets_here)
        crossing = jnp.where((step == 1) | (step == 2), 1, 0)
        left_crossing = jnp.where(step == 3, 0, jnp.where(step == 1, 2, 1))
        low = jnp.where(from_right, PER - crossing, jnp.where(with_own, PER, 2 * PER))
        high = jnp.where(from_right, jnp.where(with_own, 2 * PER, PER), 2 * PER + left_crossing)

        @pl.when((step < PER - 1) | with_own)
        def _():
            def one(chunk, inner):
                arrived(step, chunk, side, slot).wait_recv()
                normalise(slot, chunk)
                meet(slot, chunk, low, high)
                return inner

            lax.fori_loop(0, chunks, one, 0)

        return carry

    lax.fori_loop(0, 2 * PER, exchange_step, 0)

    def best_of(slot):
        return jnp.maximum(row_best[slot, 0:1, :], jnp.max(col_best[slot], axis=0, keepdims=True))

    for block in range(PER):
        sent_best[0, block : block + 1, :] = best_of(block)
        sent_best[1, block : block + 1, :] = best_of(2 * PER + block)
    best_left = pltpu.make_async_remote_copy(
        src_ref=sent_best.at[0], dst_ref=got_best.at[0], send_sem=best_send.at[0], recv_sem=best_recv.at[0],
        device_id=left, device_id_type=MESH,
    )
    best_right = pltpu.make_async_remote_copy(
        src_ref=sent_best.at[1], dst_ref=got_best.at[1], send_sem=best_send.at[1], recv_sem=best_recv.at[1],
        device_id=right, device_id_type=MESH,
    )
    best_left.start()
    best_right.start()

    for step in range(PER - 1):
        for chunk in range(chunks):
            push(step, chunk, True).wait_send()
            push(step, chunk, False).wait_send()

    @pl.when(sends_last_left)
    def _():
        for chunk in range(chunks):
            push(PER - 1, chunk, True).wait_send()

    @pl.when(sends_last_right)
    def _():
        for chunk in range(chunks):
            push(PER - 1, chunk, False).wait_send()

    best_left.wait()
    best_right.wait()
    ids = lax.broadcasted_iota(jnp.int32, (1, rows_all), 1)
    for block in range(PER):
        best = jnp.maximum(best_of(PER + block), jnp.float32(-1.0))
        best = jnp.maximum(best, got_best[0, block : block + 1, :])
        best = jnp.maximum(best, got_best[1, block : block + 1, :])
        out[block : block + 1, :] = jnp.where(ids < counts[block], best, jnp.float32(0.0))


def solution(mesh):
    devices = mesh.size

    def per_device(embeddings, partners, cluster, counts):
        blocks, rows, width = embeddings.shape
        chunks = rows // CHUNK
        return pl.pallas_call(
            functools.partial(kernel, devices),
            out_shape=jax.ShapeDtypeStruct((blocks, rows), jnp.float32),
            in_specs=[
                pl.BlockSpec(memory_space=pl.ANY),
                pl.BlockSpec(memory_space=pltpu.VMEM),
                pl.BlockSpec(memory_space=pltpu.SMEM),
                pl.BlockSpec(memory_space=pltpu.SMEM),
            ],
            out_specs=pl.BlockSpec(memory_space=pltpu.VMEM),
            scratch_shapes=[
                pltpu.VMEM((3 * PER, rows, width), jnp.bfloat16),
                pltpu.VMEM((3, 16, 128), jnp.int32),
                pltpu.SMEM((3, 16, 128), jnp.int32),
                pltpu.VMEM((3 * PER, 8, rows), jnp.float32),
                pltpu.VMEM((CHUNK, 128), jnp.float32),
                pltpu.VMEM((3 * PER, 8, rows), jnp.float32),
                pltpu.VMEM((2, PER, rows), jnp.float32),
                pltpu.VMEM((2, PER, rows), jnp.float32),
                pltpu.SemaphoreType.DMA((PER,)),
                pltpu.SemaphoreType.DMA((2, PER, chunks)),
                pltpu.SemaphoreType.DMA((2, PER, chunks)),
                pltpu.SemaphoreType.DMA((2,)),
                pltpu.SemaphoreType.DMA((2,)),
                pltpu.SemaphoreType.DMA,
                pltpu.SemaphoreType.DMA((2,)),
                pltpu.SemaphoreType.DMA((2,)),
            ],
            compiler_params=pltpu.CompilerParams(
                collective_id=0, has_side_effects=True, vmem_limit_bytes=40 * 2**20
            ),
        )(embeddings, partners, cluster, counts)

    return jax.shard_map(
        per_device,
        mesh=mesh,
        in_specs=(P(AXES, None, None), P(AXES, None), P(AXES), P(AXES)),
        out_specs=P(AXES, None),
        check_vma=False,
    )
```

```python
import jax
import jax.numpy as jnp
from jax import lax
from jax.experimental import pallas as pl
from jax.experimental.pallas import tpu as pltpu
from jax.sharding import PartitionSpec as P

MESH = pl.DeviceIdType.MESH
AXES = ("shard", "group")
PER = 4
SLOTS = 3 * PER
HALF = 256
LOW = -4.0
LEFT, OWN, RIGHT, MATE_R, MATE_L, BEHIND, AHEAD = range(7)
NEAR, NEXT, THIRD, FOURTH = range(4)
PIECES = ((0, HALF), (HALF, HALF))


def fold_rows(scores):
    rows, columns = scores.shape
    return jnp.max(scores.reshape(rows // 8, 8, columns), axis=0)


def fold_columns(scores):
    best = scores[:, 0:128]
    for start in range(128, scores.shape[1], 128):
        best = jnp.maximum(best, scores[:, start : start + 128])
    return best


def kernel(
    emb,
    partners_hbm,
    cluster_hbm,
    counts_hbm,
    out,
    window,
    raw,
    stage,
    swapped,
    partners,
    cluster,
    counts,
    info,
    facts,
    col_best,
    row_part,
    row_best,
    sent_best,
    got_best,
    load_sem,
    small_sem,
    stage_sem,
    emb_send,
    emb_recv,
    swap_send,
    swap_recv,
    pass_send,
    pass_recv,
    info_send,
    info_recv,
    facts_sem,
    best_send,
    best_recv,
):
    rows_all = window.shape[1]
    shards = lax.axis_size("shard")
    groups = lax.axis_size("group")
    total = shards * groups
    pool = 2 * groups
    me = lax.axis_index("shard") * groups + lax.axis_index("group")

    def place(index):
        index = lax.rem(index + total, total)
        return (lax.div(index, groups), lax.rem(index, groups))

    first_r = lax.rem(me, pool) < groups
    first_l = lax.rem(me + total - 1, pool) < groups
    mate_r = jnp.where(first_r, me + groups, me - groups)
    mate_l = jnp.where(first_l, me + groups, me - groups)
    where_is = {
        LEFT: place(me - 1),
        RIGHT: place(me + 1),
        MATE_R: place(mate_r),
        MATE_L: place(mate_l),
        BEHIND: place(mate_l - 1),
        AHEAD: place(mate_r + 1),
    }
    seen_as = {LEFT: RIGHT, RIGHT: LEFT, MATE_R: MATE_R, MATE_L: MATE_L, BEHIND: AHEAD, AHEAD: BEHIND}

    barrier = pltpu.get_barrier_semaphore()
    for role in where_is:
        pl.semaphore_signal(barrier, inc=1, device_id=where_is[role], device_id_type=MESH)

    small = [
        pltpu.make_async_copy(partners_hbm, partners, small_sem.at[0]),
        pltpu.make_async_copy(cluster_hbm, cluster, small_sem.at[1]),
        pltpu.make_async_copy(counts_hbm, counts, small_sem.at[2]),
    ]
    loads = [pltpu.make_async_copy(emb.at[block], window.at[PER + block], load_sem.at[block]) for block in range(PER)]
    stages = [
        pltpu.make_async_copy(emb.at[2], stage.at[0], stage_sem.at[0]),
        pltpu.make_async_copy(emb.at[1], stage.at[1], stage_sem.at[1]),
    ]
    for copy in small + loads + stages:
        copy.start()
    info[OWN] = jnp.zeros(info.shape[1:], jnp.int32)
    for copy in small:
        copy.wait()
    info[OWN, 0:PER, 0 : partners.shape[1]] = partners[...]
    for block in range(PER):
        info[OWN, PER + block : PER + block + 1, :] = jnp.full((1, 128), cluster[block], jnp.int32)
        info[OWN, 2 * PER + block : 2 * PER + block + 1, :] = jnp.full((1, 128), counts[block], jnp.int32)
    pl.semaphore_wait(barrier, len(where_is))

    def remote(source, target, send_sem, recv_sem, role):
        return pltpu.make_async_remote_copy(
            src_ref=source,
            dst_ref=target,
            send_sem=send_sem,
            recv_sem=recv_sem,
            device_id=where_is[role],
            device_id_type=MESH,
        )

    def push(step, side, piece):
        start, size = PIECES[piece]
        rows = pl.ds(start, size)
        block = step if side == 0 else PER - 1 - step
        source = stage.at[side, rows, :] if step == THIRD else emb.at[block, rows, :]
        return remote(
            source,
            raw.at[side, step, rows, :],
            emb_send.at[side, step, piece],
            emb_recv.at[side, step, piece],
            LEFT if side == 0 else RIGHT,
        )

    def pass_on(side, piece):
        rows = pl.ds(*PIECES[piece])
        return remote(
            raw.at[side, THIRD, rows, :],
            raw.at[side, FOURTH, rows, :],
            pass_send.at[side, piece],
            pass_recv.at[side, piece],
            MATE_R if side == 0 else MATE_L,
        )

    infos = [
        remote(info.at[OWN], info.at[seen_as[role]], info_send.at[role], info_recv.at[seen_as[role]], role)
        for role in where_is
    ]

    def swap(side, piece):
        rows = pl.ds(*PIECES[piece])
        return remote(
            emb.at[PER - 1 if side == 0 else 0, rows, :],
            swapped.at[side, rows, :],
            swap_send.at[side, piece],
            swap_recv.at[side, piece],
            MATE_L if side == 0 else MATE_R,
        )

    for copy in infos:
        copy.start()
    for piece in range(len(PIECES)):
        for side in range(2):
            swap(side, piece).start()

    for piece in range(len(PIECES)):
        for side in range(2):
            push(NEAR, side, piece).start()

    col_best[...] = jnp.full(col_best.shape, LOW, jnp.float32)
    row_best[...] = jnp.full(row_best.shape, LOW, jnp.float32)
    for copy in infos:
        copy.wait()
    to_facts = pltpu.make_async_copy(info, facts, facts_sem)
    to_facts.start()
    for copy in loads + stages:
        copy.wait()
    to_facts.wait()

    def cluster_of(device, block):
        return facts[device, PER + block, 0]

    def spans(device_a, device_b):
        head = cluster_of(device_a, 0)
        return head == cluster_of(device_b, 3), head == cluster_of(device_b, 2)

    def third_is_lent(is_first, spans_all, spans_three, mate_spans_all):
        keeps_left = spans_three & (is_first | jnp.logical_not(spans_all))
        return mate_spans_all & jnp.logical_not(keeps_left), mate_spans_all & keeps_left

    whole_r, three_r = spans(OWN, RIGHT)
    whole_mr, three_mr = spans(MATE_R, AHEAD)
    whole_l, three_l = spans(LEFT, OWN)
    whole_ml, three_ml = spans(BEHIND, MATE_L)
    r_left, r_right = third_is_lent(first_r, whole_r, three_r, whole_mr)
    mr_left, _ = third_is_lent(jnp.logical_not(first_r), whole_mr, three_mr, whole_r)
    l_left, l_right = third_is_lent(first_l, whole_l, three_l, whole_ml)
    _, ml_right = third_is_lent(jnp.logical_not(first_l), whole_ml, three_ml, whole_l)

    def slot_cost(slot):
        holds = jnp.where(slot == 2 * PER + THIRD, jnp.logical_not(r_left), True)
        holds = jnp.where(slot == 2 * PER + FOURTH, mr_left, holds)
        holds = jnp.where(slot == PER - 1 - THIRD, jnp.logical_not(l_right), holds)
        return jnp.where(slot == PER - 1 - FOURTH, ml_right, holds)

    def count_of(slot):
        return facts[lax.div(slot, PER), 2 * PER + lax.rem(slot, PER), 0]

    def penalty(slot, other):
        first, second = jnp.minimum(slot, other), jnp.maximum(slot, other)
        device_a, block_a = lax.div(first, PER), lax.rem(first, PER)
        device_b, block_b = lax.div(second, PER), lax.rem(second, PER)
        listed = facts[device_a, block_a, second - first] >= 0
        same = cluster_of(device_a, block_a) == cluster_of(device_b, block_b)
        held = slot_cost(slot) & slot_cost(other)
        return jnp.where(listed & same & held, jnp.float32(0.0), jnp.float32(LOW))

    def normalise(slot, start, size, load):
        rows = pl.ds(start, size)
        floats = load(rows).astype(jnp.float32)
        unit = floats * lax.rsqrt(jnp.sum(floats * floats, axis=-1, keepdims=True) + 1e-06)
        head = window[slot, 0:16, :].astype(jnp.float32)[0:1, :]
        head = jnp.where(start == 0, unit[0:1, :], head)
        ids = start + lax.broadcasted_iota(jnp.int32, (size, 1), 0)
        window[slot, rows, :] = jnp.where(ids < count_of(slot), unit, head).astype(jnp.bfloat16)

    def scored(slot, rows, other, columns):
        return lax.dot_general(
            window[slot, rows, :],
            window[other, columns, :],
            (((1,), (1,)), ((), ())),
            preferred_element_type=jnp.float32,
        )

    def meet_one(slot, rows, part, other, columns):
        scores = scored(slot, rows, other, columns)
        cost = penalty(slot, other)
        col_best[other, :, columns] = jnp.maximum(col_best[other, :, columns], fold_rows(scores) + cost)
        part[...] = jnp.maximum(part[...], fold_columns(scores) + cost)

    def meet(slot, start, size, low, high, halves=(), unroll=False):
        rows, every = pl.ds(start, size), pl.ds(0, rows_all)
        part = row_part.at[0:size, :]
        part[...] = jnp.full((size, 128), LOW, jnp.float32)
        for other in halves:
            meet_one(slot, rows, part, other, pl.ds(0, HALF))
        if unroll:
            for other in range(low, high):
                meet_one(slot, rows, part, other, every)
        else:

            def one(other, carry):
                meet_one(slot, rows, part, other, every)
                return carry

            lax.fori_loop(low, high, one, 0)
        best = jnp.max(part[...].T, axis=0, keepdims=True)
        row_best[slot, :, rows] = jnp.broadcast_to(best, (8, size))

    def own_normalise(index, carry):
        slot, start = PER + lax.div(index, 2), pl.multiple_of(lax.rem(index, 2) * HALF, HALF)
        normalise(slot, start, HALF, lambda rows: window[slot, rows, :])
        return carry

    lax.fori_loop(0, PER * 2, own_normalise, 0)

    def own_step(slot, carry):
        meet(slot, 0, rows_all, PER, slot)
        scores = scored(slot, pl.ds(0, rows_all), slot, pl.ds(0, rows_all))
        row_ids = lax.broadcasted_iota(jnp.int32, scores.shape, 0)
        col_ids = lax.broadcasted_iota(jnp.int32, scores.shape, 1)
        allowed = (row_ids < count_of(slot)) & (row_ids != col_ids)
        scores = jnp.where(allowed, scores, jnp.float32(LOW))
        col_best[slot] = jnp.maximum(col_best[slot], fold_rows(scores) + penalty(slot, slot))
        return carry

    lax.fori_loop(PER, 2 * PER, own_step, 0)

    for piece, (first, size) in enumerate(PIECES):
        for side, lent in ((0, l_left), (1, r_right)):
            swap(side, piece).wait()

            def choose(index, carry, side=side, lent=lent, first=first):
                rows = pl.ds(pl.multiple_of(first + index * 64, 64), 64)
                stage[side, rows, :] = jnp.where(lent, swapped[side, rows, :], stage[side, rows, :])
                return carry

            lax.fori_loop(0, size // 64, choose, 0)
            push(THIRD, side, piece).start()

    def take(step, side, pieces, low, high, halves=(), unroll=False):
        slot = 2 * PER + step if side == 0 else PER - 1 - step
        for piece in pieces:
            if step == FOURTH:
                pass_on(side, piece).wait_recv()
            elif step != THIRD:
                push(step, side, piece).wait_recv()
            normalise(slot, *PIECES[piece], lambda rows: raw[side, step, rows, :])
        start, size = PIECES[pieces[0]][0], sum(PIECES[piece][1] for piece in pieces)
        meet(slot, start, size, low, high, halves, unroll)

    both = (0, 1)
    own, right, left_next, right_next = PER, 2 * PER, PER - 1 - NEXT, 2 * PER + NEXT
    take(NEAR, 0, both, own, right)
    take(NEAR, 1, both, own + 1, right + 1)
    for piece in both:
        for side in (1, 0):
            push(THIRD, side, piece).wait_recv()
            pass_on(side, piece).start()
            push(NEXT, side, piece).start()
    take(THIRD, 0, both, own - 1, right)
    take(THIRD, 1, both, own + 2, right + 1)
    take(NEXT, 0, (0,), own - 1, right - 1)
    take(NEXT, 1, (0,), own + 2, right + 1, (right_next,))
    take(FOURTH, 0, both, own, own + 2)
    take(FOURTH, 1, both, own + 2, right)
    take(NEXT, 0, (1,), own - 1, right - 1, (left_next,), True)
    take(NEXT, 1, (1,), own + 2, right + 2, (), True)

    def best_of(slot):
        return jnp.maximum(row_best[slot, 0:1, :], jnp.max(col_best[slot], axis=0, keepdims=True))

    for block in range(PER):
        sent_best[0, block : block + 1, :] = best_of(block)
        sent_best[1, block : block + 1, :] = best_of(2 * PER + block)
    bests = [
        remote(sent_best.at[0], got_best.at[0], best_send.at[0], best_recv.at[0], LEFT),
        remote(sent_best.at[1], got_best.at[1], best_send.at[1], best_recv.at[1], RIGHT),
    ]
    for copy in bests:
        copy.start()

    for step in (NEAR, NEXT, THIRD):
        for piece in range(len(PIECES)):
            for side in range(2):
                push(step, side, piece).wait_send()
    for side in range(2):
        for piece in range(len(PIECES)):
            pass_on(side, piece).wait_send()

    for copy in bests:
        copy.wait()
    ids = lax.broadcasted_iota(jnp.int32, (1, rows_all), 1)
    for block in range(PER):
        best = jnp.maximum(best_of(PER + block), jnp.float32(-1.0))
        best = jnp.maximum(best, got_best[0, block : block + 1, :])
        best = jnp.maximum(best, got_best[1, block : block + 1, :])
        out[block : block + 1, :] = jnp.where(ids < counts[block], best, jnp.float32(0.0))


def solution(mesh):
    def per_device(embeddings, partners, cluster, counts):
        blocks, rows, width = embeddings.shape
        dma = pltpu.SemaphoreType.DMA
        return pl.pallas_call(
            kernel,
            out_shape=jax.ShapeDtypeStruct((blocks, rows), jnp.float32),
            in_specs=[pl.BlockSpec(memory_space=pl.ANY)] * 4,
            out_specs=pl.BlockSpec(memory_space=pltpu.VMEM),
            scratch_shapes=[
                pltpu.VMEM((SLOTS, rows, width), jnp.bfloat16),
                pltpu.VMEM((2, PER, rows, width), jnp.bfloat16),
                pltpu.VMEM((2, rows, width), jnp.bfloat16),
                pltpu.VMEM((2, rows, width), jnp.bfloat16),
                pltpu.VMEM(partners.shape, jnp.int32),
                pltpu.SMEM(cluster.shape, jnp.int32),
                pltpu.SMEM(counts.shape, jnp.int32),
                pltpu.VMEM((7, 16, 128), jnp.int32),
                pltpu.SMEM((7, 16, 128), jnp.int32),
                pltpu.VMEM((SLOTS, 8, rows), jnp.float32),
                pltpu.VMEM((rows, 128), jnp.float32),
                pltpu.VMEM((SLOTS, 8, rows), jnp.float32),
                pltpu.VMEM((2, PER, rows), jnp.float32),
                pltpu.VMEM((2, PER, rows), jnp.float32),
                dma((PER,)),
                dma((3,)),
                dma((2,)),
                dma((2, 3, 2)),
                dma((2, 3, 2)),
                dma((2, 2)),
                dma((2, 2)),
                dma((2, 2)),
                dma((2, 2)),
                dma((7,)),
                dma((7,)),
                dma,
                dma((2,)),
                dma((2,)),
            ],
            compiler_params=pltpu.CompilerParams(
                collective_id=0, has_side_effects=True, vmem_limit_bytes=60 * 2**20
            ),
        )(embeddings, partners, cluster, counts)

    return jax.shard_map(
        per_device,
        mesh=mesh,
        in_specs=(P(AXES, None, None), P(AXES, None), P(AXES), P(AXES)),
        out_specs=P(AXES, None),
        check_vma=False,
    )
```

```python
import jax
import jax.numpy as jnp
from jax import lax
from jax.experimental import pallas as pl
from jax.experimental.pallas import tpu as pltpu
from jax.sharding import PartitionSpec as P

MESH = pl.DeviceIdType.MESH
AXES = ("shard", "group")
PER = 4
SLOTS = 3 * PER
HALF = 256
LOW = -4.0
LEFT, OWN, RIGHT, MATE_R, MATE_L, BEHIND, AHEAD = range(7)
NEAR, NEXT, THIRD, FOURTH = range(4)
PIECES = ((0, HALF), (HALF, HALF))
LAP = 64


def fold_rows(scores):
    rows, columns = scores.shape
    return jnp.max(scores.reshape(rows // 8, 8, columns), axis=0)


def fold_columns(scores):
    best = scores[:, 0:128]
    for start in range(128, scores.shape[1], 128):
        best = jnp.maximum(best, scores[:, start : start + 128])
    return best


def kernel(
    emb,
    partners_hbm,
    cluster_hbm,
    counts_hbm,
    out,
    window,
    raw,
    stage,
    swapped,
    partners,
    cluster,
    counts,
    info,
    own_facts,
    facts,
    col_best,
    row_part,
    row_best,
    sent_best,
    got_best,
    load_sem,
    small_sem,
    stage_sem,
    emb_send,
    emb_recv,
    swap_send,
    swap_recv,
    pass_send,
    pass_recv,
    info_send,
    info_recv,
    own_facts_sem,
    facts_sem,
    late_sem,
    best_send,
    best_recv,
):
    rows_all = window.shape[1]
    shards = lax.axis_size("shard")
    groups = lax.axis_size("group")
    total = shards * groups
    pool = 2 * groups
    me = lax.axis_index("shard") * groups + lax.axis_index("group")

    def place(index):
        index = lax.rem(index + total, total)
        return (lax.div(index, groups), lax.rem(index, groups))

    first_r = lax.rem(me, pool) < groups
    first_l = lax.rem(me + total - 1, pool) < groups
    mate_r = jnp.where(first_r, me + groups, me - groups)
    mate_l = jnp.where(first_l, me + groups, me - groups)
    where_is = {
        LEFT: place(me - 1),
        RIGHT: place(me + 1),
        MATE_R: place(mate_r),
        MATE_L: place(mate_l),
        BEHIND: place(mate_l - 1),
        AHEAD: place(mate_r + 1),
    }
    opens_lap = lax.rem(me, LAP) == 0
    late_for = {
        RIGHT: lax.rem(me, LAP) == LAP - 1,
        MATE_L: lax.rem(me, LAP) == LAP - groups,
        AHEAD: lax.rem(me, LAP) == LAP - 1 - groups,
    }
    seen_as = {LEFT: RIGHT, RIGHT: LEFT, MATE_R: MATE_R, MATE_L: MATE_L, BEHIND: AHEAD, AHEAD: BEHIND}

    barrier = pltpu.get_barrier_semaphore()
    for role in where_is:
        if role in late_for:

            @pl.when(jnp.logical_not(late_for[role]))
            def _(role=role):
                pl.semaphore_signal(barrier, inc=1, device_id=where_is[role], device_id_type=MESH)
        else:
            pl.semaphore_signal(barrier, inc=1, device_id=where_is[role], device_id_type=MESH)

    small = [
        pltpu.make_async_copy(partners_hbm, partners, small_sem.at[0]),
        pltpu.make_async_copy(cluster_hbm, cluster, small_sem.at[1]),
        pltpu.make_async_copy(counts_hbm, counts, small_sem.at[2]),
    ]
    loads = [pltpu.make_async_copy(emb.at[block], window.at[PER + block], load_sem.at[block]) for block in range(PER)]
    stages = [
        pltpu.make_async_copy(emb.at[2], stage.at[0], stage_sem.at[0]),
        pltpu.make_async_copy(emb.at[1], stage.at[1], stage_sem.at[1]),
    ]
    for copy in small + loads + stages:
        copy.start()
    info[OWN] = jnp.zeros(info.shape[1:], jnp.int32)
    for copy in small:
        copy.wait()
    info[OWN, 0:PER, 0 : partners.shape[1]] = partners[...]
    for block in range(PER):
        info[OWN, PER + block : PER + block + 1, :] = jnp.full((1, 128), cluster[block], jnp.int32)
        info[OWN, 2 * PER + block : 2 * PER + block + 1, :] = jnp.full((1, 128), counts[block], jnp.int32)
    to_own_facts = pltpu.make_async_copy(info.at[OWN], own_facts, own_facts_sem)
    to_own_facts.start()
    pl.semaphore_wait(barrier, jnp.where(opens_lap, len(where_is) - len(late_for), len(where_is)))
    for role in late_for:

        @pl.when(late_for[role])
        def _(role=role):
            pl.semaphore_signal(late_sem, inc=1, device_id=where_is[role], device_id_type=MESH)

    def remote(source, target, send_sem, recv_sem, role):
        return pltpu.make_async_remote_copy(
            src_ref=source,
            dst_ref=target,
            send_sem=send_sem,
            recv_sem=recv_sem,
            device_id=where_is[role],
            device_id_type=MESH,
        )

    def push(step, side, piece):
        start, size = PIECES[piece]
        rows = pl.ds(start, size)
        block = step if side == 0 else PER - 1 - step
        source = stage.at[side, rows, :] if step == THIRD else emb.at[block, rows, :]
        return remote(
            source,
            raw.at[side, step, rows, :],
            emb_send.at[side, step, piece],
            emb_recv.at[side, step, piece],
            LEFT if side == 0 else RIGHT,
        )

    def pass_on(side, piece):
        rows = pl.ds(*PIECES[piece])
        return remote(
            raw.at[side, THIRD, rows, :],
            raw.at[side, FOURTH, rows, :],
            pass_send.at[side, piece],
            pass_recv.at[side, piece],
            MATE_R if side == 0 else MATE_L,
        )

    def swap(side, piece):
        rows = pl.ds(*PIECES[piece])
        return remote(
            emb.at[PER - 1 if side == 0 else 0, rows, :],
            swapped.at[side, rows, :],
            swap_send.at[side, piece],
            swap_recv.at[side, piece],
            MATE_L if side == 0 else MATE_R,
        )

    infos = {
        role: remote(info.at[OWN], info.at[seen_as[role]], info_send.at[role], info_recv.at[seen_as[role]], role)
        for role in where_is
    }
    for role in (RIGHT, MATE_R, AHEAD):
        infos[role].start()
    for piece in range(len(PIECES)):
        swap(1, piece).start()
    push(NEAR, 1, 0).start()

    @pl.when(opens_lap)
    def _():
        pl.semaphore_wait(late_sem, len(late_for))

    for role in (LEFT, MATE_L, BEHIND):
        infos[role].start()
    for piece in range(len(PIECES)):
        swap(0, piece).start()
    push(NEAR, 0, 0).start()
    push(NEAR, 1, 1).start()
    push(NEAR, 0, 1).start()

    col_best[...] = jnp.full(col_best.shape, LOW, jnp.float32)
    row_best[...] = jnp.full(row_best.shape, LOW, jnp.float32)
    for copy in loads + stages:
        copy.wait()
    to_own_facts.wait()

    def cluster_of(device, block):
        return facts[device, PER + block, 0]

    def spans(device_a, device_b):
        head = cluster_of(device_a, 0)
        return head == cluster_of(device_b, 3), head == cluster_of(device_b, 2)

    def third_is_lent(is_first, spans_all, spans_three, mate_spans_all):
        keeps_left = spans_three & (is_first | jnp.logical_not(spans_all))
        return mate_spans_all & jnp.logical_not(keeps_left), mate_spans_all & keeps_left

    def slot_cost(slot):
        holds = jnp.where(slot == 2 * PER + THIRD, jnp.logical_not(r_left), True)
        holds = jnp.where(slot == 2 * PER + FOURTH, mr_left, holds)
        holds = jnp.where(slot == PER - 1 - THIRD, jnp.logical_not(l_right), holds)
        return jnp.where(slot == PER - 1 - FOURTH, ml_right, holds)

    def count_of(slot):
        return facts[lax.div(slot, PER), 2 * PER + lax.rem(slot, PER), 0]

    def penalty(slot, other):
        first, second = jnp.minimum(slot, other), jnp.maximum(slot, other)
        device_a, block_a = lax.div(first, PER), lax.rem(first, PER)
        device_b, block_b = lax.div(second, PER), lax.rem(second, PER)
        listed = facts[device_a, block_a, second - first] >= 0
        same = cluster_of(device_a, block_a) == cluster_of(device_b, block_b)
        held = slot_cost(slot) & slot_cost(other)
        return jnp.where(listed & same & held, jnp.float32(0.0), jnp.float32(LOW))

    def own_count(slot):
        return own_facts[2 * PER + slot - PER, 0]

    def own_penalty(slot, other):
        listed = own_facts[other - PER, slot - other] >= 0
        same = own_facts[slot, 0] == own_facts[other, 0]
        return jnp.where(listed & same, jnp.float32(0.0), jnp.float32(LOW))

    def normalise(slot, start, size, load, count):
        rows = pl.ds(start, size)
        floats = load(rows).astype(jnp.float32)
        unit = floats * lax.rsqrt(jnp.sum(floats * floats, axis=-1, keepdims=True) + 1e-06)
        head = window[slot, 0:16, :].astype(jnp.float32)[0:1, :]
        head = jnp.where(start == 0, unit[0:1, :], head)
        ids = start + lax.broadcasted_iota(jnp.int32, (size, 1), 0)
        window[slot, rows, :] = jnp.where(ids < count, unit, head).astype(jnp.bfloat16)

    def scored(slot, rows, other, columns):
        return lax.dot_general(
            window[slot, rows, :],
            window[other, columns, :],
            (((1,), (1,)), ((), ())),
            preferred_element_type=jnp.float32,
        )

    def meet_one(slot, rows, part, other, columns, cost):
        scores = scored(slot, rows, other, columns)
        col_best[other, :, columns] = jnp.maximum(col_best[other, :, columns], fold_rows(scores) + cost)
        part[...] = jnp.maximum(part[...], fold_columns(scores) + cost)

    def meet(slot, start, size, low, high, halves=(), unroll=False, cost=penalty):
        rows, every = pl.ds(start, size), pl.ds(0, rows_all)
        part = row_part.at[0:size, :]
        part[...] = jnp.full((size, 128), LOW, jnp.float32)
        for other in halves:
            meet_one(slot, rows, part, other, pl.ds(0, HALF), cost(slot, other))
        if unroll:
            for other in range(low, high):
                meet_one(slot, rows, part, other, every, cost(slot, other))
        else:

            def one(other, carry):
                meet_one(slot, rows, part, other, every, cost(slot, other))
                return carry

            lax.fori_loop(low, high, one, 0)
        best = jnp.max(part[...].T, axis=0, keepdims=True)
        row_best[slot, :, rows] = jnp.broadcast_to(best, (8, size))

    def own_normalise(index, carry):
        slot, start = PER + lax.div(index, 2), pl.multiple_of(lax.rem(index, 2) * HALF, HALF)
        normalise(slot, start, HALF, lambda rows: window[slot, rows, :], own_count(slot))
        return carry

    lax.fori_loop(0, PER * 2, own_normalise, 0)

    def own_step(slot, carry):
        meet(slot, 0, rows_all, PER, slot, cost=own_penalty)
        scores = scored(slot, pl.ds(0, rows_all), slot, pl.ds(0, rows_all))
        row_ids = lax.broadcasted_iota(jnp.int32, scores.shape, 0)
        col_ids = lax.broadcasted_iota(jnp.int32, scores.shape, 1)
        allowed = (row_ids < own_count(slot)) & (row_ids != col_ids)
        scores = jnp.where(allowed, scores, jnp.float32(LOW))
        col_best[slot] = jnp.maximum(col_best[slot], fold_rows(scores) + own_penalty(slot, slot))
        return carry

    lax.fori_loop(PER, 2 * PER, own_step, 0)

    for role in infos:
        infos[role].wait()
    to_facts = pltpu.make_async_copy(info, facts, facts_sem)
    to_facts.start()
    to_facts.wait()
    whole_r, three_r = spans(OWN, RIGHT)
    whole_mr, three_mr = spans(MATE_R, AHEAD)
    whole_l, three_l = spans(LEFT, OWN)
    whole_ml, three_ml = spans(BEHIND, MATE_L)
    r_left, r_right = third_is_lent(first_r, whole_r, three_r, whole_mr)
    mr_left, _ = third_is_lent(jnp.logical_not(first_r), whole_mr, three_mr, whole_r)
    l_left, l_right = third_is_lent(first_l, whole_l, three_l, whole_ml)
    _, ml_right = third_is_lent(jnp.logical_not(first_l), whole_ml, three_ml, whole_l)

    for piece, (first, size) in enumerate(PIECES):
        for side, lent in ((0, l_left), (1, r_right)):
            swap(side, piece).wait()

            def choose(index, carry, side=side, lent=lent, first=first):
                rows = pl.ds(pl.multiple_of(first + index * 64, 64), 64)
                stage[side, rows, :] = jnp.where(lent, swapped[side, rows, :], stage[side, rows, :])
                return carry

            lax.fori_loop(0, size // 64, choose, 0)
            push(THIRD, side, piece).start()

    def take(step, side, pieces, low, high, halves=(), unroll=False):
        slot = 2 * PER + step if side == 0 else PER - 1 - step
        for piece in pieces:
            if step == FOURTH:
                pass_on(side, piece).wait_recv()
            elif step != THIRD:
                push(step, side, piece).wait_recv()
            normalise(slot, *PIECES[piece], lambda rows: raw[side, step, rows, :], count_of(slot))
        start, size = PIECES[pieces[0]][0], sum(PIECES[piece][1] for piece in pieces)
        meet(slot, start, size, low, high, halves, unroll)

    both = (0, 1)
    own, right, left_next, right_next = PER, 2 * PER, PER - 1 - NEXT, 2 * PER + NEXT
    take(NEAR, 0, both, own, right)
    take(NEAR, 1, both, own + 1, right + 1)
    for piece in both:
        for side in (1, 0):
            push(THIRD, side, piece).wait_recv()
            pass_on(side, piece).start()
            push(NEXT, side, piece).start()
        take(THIRD, 0, (piece,), own - 1, right, (), True)
        take(THIRD, 1, (piece,), own + 2, right + 1, (), True)
    take(FOURTH, 0, (0,), own, own + 2, (), True)
    take(FOURTH, 1, (0,), own + 2, right, (), True)
    take(NEXT, 0, (0,), own - 1, right - 1, (), True)
    take(NEXT, 1, (0,), own + 2, right + 1, (right_next,), True)
    take(FOURTH, 0, (1,), own, own + 2, (), True)
    take(FOURTH, 1, (1,), own + 2, right, (), True)
    take(NEXT, 0, (1,), own - 1, right - 1, (left_next,), True)
    take(NEXT, 1, (1,), own + 2, right + 2, (), True)

    def best_of(slot):
        return jnp.maximum(row_best[slot, 0:1, :], jnp.max(col_best[slot], axis=0, keepdims=True))

    for block in range(PER):
        sent_best[0, block : block + 1, :] = best_of(block)
        sent_best[1, block : block + 1, :] = best_of(2 * PER + block)
    bests = [
        remote(sent_best.at[0], got_best.at[0], best_send.at[0], best_recv.at[0], LEFT),
        remote(sent_best.at[1], got_best.at[1], best_send.at[1], best_recv.at[1], RIGHT),
    ]
    for copy in bests:
        copy.start()

    for step in (NEAR, NEXT, THIRD):
        for piece in range(len(PIECES)):
            for side in range(2):
                push(step, side, piece).wait_send()
    for side in range(2):
        for piece in range(len(PIECES)):
            pass_on(side, piece).wait_send()

    for copy in bests:
        copy.wait()
    ids = lax.broadcasted_iota(jnp.int32, (1, rows_all), 1)
    for block in range(PER):
        best = jnp.maximum(best_of(PER + block), jnp.float32(-1.0))
        best = jnp.maximum(best, got_best[0, block : block + 1, :])
        best = jnp.maximum(best, got_best[1, block : block + 1, :])
        out[block : block + 1, :] = jnp.where(ids < counts[block], best, jnp.float32(0.0))


def solution(mesh):
    def per_device(embeddings, partners, cluster, counts):
        blocks, rows, width = embeddings.shape
        dma = pltpu.SemaphoreType.DMA
        return pl.pallas_call(
            kernel,
            out_shape=jax.ShapeDtypeStruct((blocks, rows), jnp.float32),
            in_specs=[pl.BlockSpec(memory_space=pl.ANY)] * 4,
            out_specs=pl.BlockSpec(memory_space=pltpu.VMEM),
            scratch_shapes=[
                pltpu.VMEM((SLOTS, rows, width), jnp.bfloat16),
                pltpu.VMEM((2, PER, rows, width), jnp.bfloat16),
                pltpu.VMEM((2, rows, width), jnp.bfloat16),
                pltpu.VMEM((2, rows, width), jnp.bfloat16),
                pltpu.VMEM(partners.shape, jnp.int32),
                pltpu.SMEM(cluster.shape, jnp.int32),
                pltpu.SMEM(counts.shape, jnp.int32),
                pltpu.VMEM((7, 16, 128), jnp.int32),
                pltpu.SMEM((16, 128), jnp.int32),
                pltpu.SMEM((7, 16, 128), jnp.int32),
                pltpu.VMEM((SLOTS, 8, rows), jnp.float32),
                pltpu.VMEM((rows, 128), jnp.float32),
                pltpu.VMEM((SLOTS, 8, rows), jnp.float32),
                pltpu.VMEM((2, PER, rows), jnp.float32),
                pltpu.VMEM((2, PER, rows), jnp.float32),
                dma((PER,)),
                dma((3,)),
                dma((2,)),
                dma((2, 3, 2)),
                dma((2, 3, 2)),
                dma((2, 2)),
                dma((2, 2)),
                dma((2, 2)),
                dma((2, 2)),
                dma((7,)),
                dma((7,)),
                dma,
                dma,
                pltpu.SemaphoreType.REGULAR,
                dma((2,)),
                dma((2,)),
            ],
            compiler_params=pltpu.CompilerParams(
                collective_id=0, has_side_effects=True, vmem_limit_bytes=60 * 2**20
            ),
        )(embeddings, partners, cluster, counts)

    return jax.shard_map(
        per_device,
        mesh=mesh,
        in_specs=(P(AXES, None, None), P(AXES, None), P(AXES), P(AXES)),
        out_specs=P(AXES, None),
        check_vma=False,
    )
```

```python
import jax
import jax.numpy as jnp
from jax import lax
from jax.experimental import pallas as pl
from jax.experimental.pallas import tpu as pltpu
from jax.sharding import PartitionSpec as P

MESH = pl.DeviceIdType.MESH
AXES = ("shard", "group")
PER = 4
SLOTS = 3 * PER
HALF = 256
LOW = -4.0
LEFT, OWN, RIGHT, MATE_R, MATE_L, BEHIND, AHEAD = range(7)
NEAR, NEXT, THIRD, FOURTH = range(4)
PIECES = ((0, HALF), (HALF, HALF))
PARTS = ((0, HALF // 2), (HALF // 2, HALF // 2), (HALF, HALF))
LAP = 64


def fold_rows(scores):
    rows, columns = scores.shape
    return jnp.max(scores.reshape(rows // 8, 8, columns), axis=0)


def fold_columns(scores):
    best = scores[:, 0:128]
    for start in range(128, scores.shape[1], 128):
        best = jnp.maximum(best, scores[:, start : start + 128])
    return best


def kernel(
    emb,
    partners_hbm,
    cluster_hbm,
    counts_hbm,
    out,
    window,
    raw,
    stage,
    swapped,
    partners,
    cluster,
    counts,
    info,
    own_facts,
    facts,
    col_best,
    row_part,
    row_best,
    sent_best,
    got_best,
    load_sem,
    small_sem,
    stage_sem,
    emb_send,
    emb_recv,
    swap_send,
    swap_recv,
    pass_send,
    pass_recv,
    info_send,
    info_recv,
    own_facts_sem,
    facts_sem,
    late_sem,
    best_send,
    best_recv,
):
    rows_all = window.shape[1]
    shards = lax.axis_size("shard")
    groups = lax.axis_size("group")
    total = shards * groups
    pool = 2 * groups
    me = lax.axis_index("shard") * groups + lax.axis_index("group")

    def place(index):
        index = lax.rem(index + total, total)
        return (lax.div(index, groups), lax.rem(index, groups))

    first_r = lax.rem(me, pool) < groups
    first_l = lax.rem(me + total - 1, pool) < groups
    mate_r = jnp.where(first_r, me + groups, me - groups)
    mate_l = jnp.where(first_l, me + groups, me - groups)
    where_is = {
        LEFT: place(me - 1),
        RIGHT: place(me + 1),
        MATE_R: place(mate_r),
        MATE_L: place(mate_l),
        BEHIND: place(mate_l - 1),
        AHEAD: place(mate_r + 1),
    }
    opens_lap = lax.rem(me, LAP) == 0
    late_for = {
        RIGHT: lax.rem(me, LAP) == LAP - 1,
        MATE_L: lax.rem(me, LAP) == LAP - groups,
        AHEAD: lax.rem(me, LAP) == LAP - 1 - groups,
    }
    seen_as = {LEFT: RIGHT, RIGHT: LEFT, MATE_R: MATE_R, MATE_L: MATE_L, BEHIND: AHEAD, AHEAD: BEHIND}

    barrier = pltpu.get_barrier_semaphore()
    for role in where_is:
        if role in late_for:

            @pl.when(jnp.logical_not(late_for[role]))
            def _(role=role):
                pl.semaphore_signal(barrier, inc=1, device_id=where_is[role], device_id_type=MESH)
        else:
            pl.semaphore_signal(barrier, inc=1, device_id=where_is[role], device_id_type=MESH)

    small = [
        pltpu.make_async_copy(partners_hbm, partners, small_sem.at[0]),
        pltpu.make_async_copy(cluster_hbm, cluster, small_sem.at[1]),
        pltpu.make_async_copy(counts_hbm, counts, small_sem.at[2]),
    ]
    loads = [pltpu.make_async_copy(emb.at[block], window.at[PER + block], load_sem.at[block]) for block in range(PER)]
    stages = [
        pltpu.make_async_copy(emb.at[2], stage.at[0], stage_sem.at[0]),
        pltpu.make_async_copy(emb.at[1], stage.at[1], stage_sem.at[1]),
    ]
    for copy in small + loads + stages:
        copy.start()
    info[OWN] = jnp.zeros(info.shape[1:], jnp.int32)
    for copy in small:
        copy.wait()
    info[OWN, 0:PER, 0 : partners.shape[1]] = partners[...]
    for block in range(PER):
        info[OWN, PER + block : PER + block + 1, :] = jnp.full((1, 128), cluster[block], jnp.int32)
        info[OWN, 2 * PER + block : 2 * PER + block + 1, :] = jnp.full((1, 128), counts[block], jnp.int32)
    to_own_facts = pltpu.make_async_copy(info.at[OWN], own_facts, own_facts_sem)
    to_own_facts.start()
    pl.semaphore_wait(barrier, jnp.where(opens_lap, len(where_is) - len(late_for), len(where_is)))
    for role in late_for:

        @pl.when(late_for[role])
        def _(role=role):
            pl.semaphore_signal(late_sem, inc=1, device_id=where_is[role], device_id_type=MESH)

    def remote(source, target, send_sem, recv_sem, role):
        return pltpu.make_async_remote_copy(
            src_ref=source,
            dst_ref=target,
            send_sem=send_sem,
            recv_sem=recv_sem,
            device_id=where_is[role],
            device_id_type=MESH,
        )

    def push(step, side, piece):
        start, size = PARTS[piece] if step == NEXT else PIECES[piece]
        rows = pl.ds(start, size)
        block = step if side == 0 else PER - 1 - step
        source = stage.at[side, rows, :] if step == THIRD else emb.at[block, rows, :]
        return remote(
            source,
            raw.at[side, step, rows, :],
            emb_send.at[side, step, piece],
            emb_recv.at[side, step, piece],
            LEFT if side == 0 else RIGHT,
        )

    def pass_on(side, piece):
        rows = pl.ds(*PIECES[piece])
        return remote(
            raw.at[side, THIRD, rows, :],
            raw.at[side, FOURTH, rows, :],
            pass_send.at[side, piece],
            pass_recv.at[side, piece],
            MATE_R if side == 0 else MATE_L,
        )

    def swap(side, piece):
        rows = pl.ds(*PIECES[piece])
        return remote(
            emb.at[PER - 1 if side == 0 else 0, rows, :],
            swapped.at[side, rows, :],
            swap_send.at[side, piece],
            swap_recv.at[side, piece],
            MATE_L if side == 0 else MATE_R,
        )

    infos = {
        role: remote(info.at[OWN], info.at[seen_as[role]], info_send.at[role], info_recv.at[seen_as[role]], role)
        for role in where_is
    }
    for role in (RIGHT, MATE_R, AHEAD):
        infos[role].start()
    for piece in range(len(PIECES)):
        swap(1, piece).start()
    push(NEAR, 1, 0).start()

    @pl.when(opens_lap)
    def _():
        pl.semaphore_wait(late_sem, len(late_for))

    for role in (LEFT, MATE_L, BEHIND):
        infos[role].start()
    for piece in range(len(PIECES)):
        swap(0, piece).start()
    push(NEAR, 0, 0).start()
    push(NEAR, 1, 1).start()
    push(NEAR, 0, 1).start()

    col_best[...] = jnp.full(col_best.shape, LOW, jnp.float32)
    row_best[...] = jnp.full(row_best.shape, LOW, jnp.float32)
    for copy in loads + stages:
        copy.wait()
    to_own_facts.wait()

    def cluster_of(device, block):
        return facts[device, PER + block, 0]

    def spans(device_a, device_b):
        head = cluster_of(device_a, 0)
        return head == cluster_of(device_b, 3), head == cluster_of(device_b, 2)

    def third_is_lent(is_first, spans_all, spans_three, mate_spans_all):
        keeps_left = spans_three & (is_first | jnp.logical_not(spans_all))
        return mate_spans_all & jnp.logical_not(keeps_left), mate_spans_all & keeps_left

    def slot_cost(slot):
        holds = jnp.where(slot == 2 * PER + THIRD, jnp.logical_not(r_left), True)
        holds = jnp.where(slot == 2 * PER + FOURTH, mr_left, holds)
        holds = jnp.where(slot == PER - 1 - THIRD, jnp.logical_not(l_right), holds)
        return jnp.where(slot == PER - 1 - FOURTH, ml_right, holds)

    def count_of(slot):
        return facts[lax.div(slot, PER), 2 * PER + lax.rem(slot, PER), 0]

    def penalty(slot, other):
        first, second = jnp.minimum(slot, other), jnp.maximum(slot, other)
        device_a, block_a = lax.div(first, PER), lax.rem(first, PER)
        device_b, block_b = lax.div(second, PER), lax.rem(second, PER)
        listed = facts[device_a, block_a, second - first] >= 0
        same = cluster_of(device_a, block_a) == cluster_of(device_b, block_b)
        held = slot_cost(slot) & slot_cost(other)
        return jnp.where(listed & same & held, jnp.float32(0.0), jnp.float32(LOW))

    def own_count(slot):
        return own_facts[2 * PER + slot - PER, 0]

    def own_penalty(slot, other):
        listed = own_facts[other - PER, slot - other] >= 0
        same = own_facts[slot, 0] == own_facts[other, 0]
        return jnp.where(listed & same, jnp.float32(0.0), jnp.float32(LOW))

    def normalise(slot, start, size, load, count):
        rows = pl.ds(start, size)
        floats = load(rows).astype(jnp.float32)
        unit = floats * lax.rsqrt(jnp.sum(floats * floats, axis=-1, keepdims=True) + 1e-06)
        head = window[slot, 0:16, :].astype(jnp.float32)[0:1, :]
        head = jnp.where(start == 0, unit[0:1, :], head)
        ids = start + lax.broadcasted_iota(jnp.int32, (size, 1), 0)
        window[slot, rows, :] = jnp.where(ids < count, unit, head).astype(jnp.bfloat16)

    def scored(slot, rows, other, columns):
        return lax.dot_general(
            window[slot, rows, :],
            window[other, columns, :],
            (((1,), (1,)), ((), ())),
            preferred_element_type=jnp.float32,
        )

    def meet_one(slot, rows, part, other, columns, cost):
        scores = scored(slot, rows, other, columns)
        col_best[other, :, columns] = jnp.maximum(col_best[other, :, columns], fold_rows(scores) + cost)
        part[...] = jnp.maximum(part[...], fold_columns(scores) + cost)

    def meet(slot, start, size, low, high, halves=(), unroll=False, cost=penalty):
        rows, every = pl.ds(start, size), pl.ds(0, rows_all)
        part = row_part.at[0:size, :]
        part[...] = jnp.full((size, 128), LOW, jnp.float32)
        for other in halves:
            meet_one(slot, rows, part, other, pl.ds(0, HALF), cost(slot, other))
        if unroll:
            for other in range(low, high):
                meet_one(slot, rows, part, other, every, cost(slot, other))
        else:

            def one(other, carry):
                meet_one(slot, rows, part, other, every, cost(slot, other))
                return carry

            lax.fori_loop(low, high, one, 0)
        best = jnp.max(part[...].T, axis=0, keepdims=True)
        row_best[slot, :, rows] = jnp.broadcast_to(best, (8, size))

    def own_normalise(index, carry):
        slot, start = PER + lax.div(index, 2), pl.multiple_of(lax.rem(index, 2) * HALF, HALF)
        normalise(slot, start, HALF, lambda rows: window[slot, rows, :], own_count(slot))
        return carry

    lax.fori_loop(0, PER * 2, own_normalise, 0)

    def own_step(slot, carry):
        meet(slot, 0, rows_all, PER, slot, cost=own_penalty)
        scores = scored(slot, pl.ds(0, rows_all), slot, pl.ds(0, rows_all))
        row_ids = lax.broadcasted_iota(jnp.int32, scores.shape, 0)
        col_ids = lax.broadcasted_iota(jnp.int32, scores.shape, 1)
        allowed = (row_ids < own_count(slot)) & (row_ids != col_ids)
        scores = jnp.where(allowed, scores, jnp.float32(LOW))
        col_best[slot] = jnp.maximum(col_best[slot], fold_rows(scores) + own_penalty(slot, slot))
        return carry

    lax.fori_loop(PER, 2 * PER, own_step, 0)

    for role in infos:
        infos[role].wait()
    to_facts = pltpu.make_async_copy(info, facts, facts_sem)
    to_facts.start()
    to_facts.wait()
    whole_r, three_r = spans(OWN, RIGHT)
    whole_mr, three_mr = spans(MATE_R, AHEAD)
    whole_l, three_l = spans(LEFT, OWN)
    whole_ml, three_ml = spans(BEHIND, MATE_L)
    r_left, r_right = third_is_lent(first_r, whole_r, three_r, whole_mr)
    mr_left, _ = third_is_lent(jnp.logical_not(first_r), whole_mr, three_mr, whole_r)
    l_left, l_right = third_is_lent(first_l, whole_l, three_l, whole_ml)
    _, ml_right = third_is_lent(jnp.logical_not(first_l), whole_ml, three_ml, whole_l)

    same_lap = (lax.rem(me, LAP) != 0, lax.rem(me, LAP) != LAP - 1)
    goes_first = ((lax.rem(me, pool) == 0) & same_lap[0], (lax.rem(me, pool) == pool - 1) & same_lap[1])
    turns = ((lax.rem(me, groups) == 0) & same_lap[0], (lax.rem(me, groups) == groups - 1) & same_lap[1])
    both, every_part = (0, 1), (0, 1, 2)

    def push_if(condition, step, side, pieces):
        @pl.when(condition)
        def _():
            for piece in pieces:
                push(step, side, piece).start()

    for piece, (first, size) in enumerate(PIECES):
        for side, lent in ((0, l_left), (1, r_right)):
            swap(side, piece).wait()

            def choose(index, carry, side=side, lent=lent, first=first):
                rows = pl.ds(pl.multiple_of(first + index * 64, 64), 64)
                stage[side, rows, :] = jnp.where(lent, swapped[side, rows, :], stage[side, rows, :])
                return carry

            lax.fori_loop(0, size // 64, choose, 0)
            push_if(jnp.logical_not(goes_first[side]), THIRD, side, (piece,))
    for side in (0, 1):
        push_if(jnp.logical_not(goes_first[side]), NEXT, side, every_part)

    def take(step, side, pieces, low, high, halves=(), unroll=False):
        slot = 2 * PER + step if side == 0 else PER - 1 - step
        for piece in pieces:
            if step == FOURTH:
                pass_on(side, piece).wait_recv()
            elif step == NEXT:
                for part in ((0, 1), (2,))[piece]:
                    push(NEXT, side, part).wait_recv()
            normalise(slot, *PIECES[piece], lambda rows: raw[side, step, rows, :], count_of(slot))
        start, size = PIECES[pieces[0]][0], sum(PIECES[piece][1] for piece in pieces)
        meet(slot, start, size, low, high, halves, unroll)

    own, right, left_next, right_next = PER, 2 * PER, PER - 1 - NEXT, 2 * PER + NEXT
    for piece in both:
        for side in both:
            push(NEAR, side, piece).wait_recv()
    for side in both:
        push_if(goes_first[side], THIRD, side, both)
    take(NEAR, 0, both, own, right)
    take(NEAR, 1, both, own + 1, right + 1)
    for piece in both:
        for side in (1, 0):
            push(THIRD, side, piece).wait_recv()
            pass_on(side, piece).start()
        if piece == 1:
            for side in both:
                push_if(goes_first[side], NEXT, side, every_part)
        take(THIRD, 0, (piece,), own - 1, right, (), True)
        take(THIRD, 1, (piece,), own + 2, right + 1, (), True)
    take(FOURTH, 0, (0,), own, own + 2, (), True)
    take(FOURTH, 1, (0,), own + 2, right, (), True)
    take(NEXT, 0, (0,), own - 1, right - 1, (), True)
    take(NEXT, 1, (0,), own + 2, right + 1, (right_next,), True)
    take(FOURTH, 0, (1,), own, own + 2, (), True)
    take(FOURTH, 1, (1,), own + 2, right, (), True)
    take(NEXT, 0, (1,), own - 1, right - 1, (left_next,), True)
    take(NEXT, 1, (1,), own + 2, right + 2, (), True)

    def best_of(slot):
        return jnp.maximum(row_best[slot, 0:1, :], jnp.max(col_best[slot], axis=0, keepdims=True))

    for block in range(PER):
        sent_best[0, block : block + 1, :] = best_of(block)
        sent_best[1, block : block + 1, :] = best_of(2 * PER + block)
    bests = [
        remote(sent_best.at[0], got_best.at[0], best_send.at[0], best_recv.at[0], LEFT),
        remote(sent_best.at[1], got_best.at[1], best_send.at[1], best_recv.at[1], RIGHT),
    ]
    for copy in bests:
        copy.start()

    for step in (NEAR, NEXT, THIRD):
        for piece in range(len(PARTS if step == NEXT else PIECES)):
            for side in range(2):
                push(step, side, piece).wait_send()
    for side in range(2):
        for piece in range(len(PIECES)):
            pass_on(side, piece).wait_send()

    for copy in bests:
        copy.wait()
    ids = lax.broadcasted_iota(jnp.int32, (1, rows_all), 1)
    for block in range(PER):
        best = jnp.maximum(best_of(PER + block), jnp.float32(-1.0))
        best = jnp.maximum(best, got_best[0, block : block + 1, :])
        best = jnp.maximum(best, got_best[1, block : block + 1, :])
        out[block : block + 1, :] = jnp.where(ids < counts[block], best, jnp.float32(0.0))


def solution(mesh):
    def per_device(embeddings, partners, cluster, counts):
        blocks, rows, width = embeddings.shape
        dma = pltpu.SemaphoreType.DMA
        return pl.pallas_call(
            kernel,
            out_shape=jax.ShapeDtypeStruct((blocks, rows), jnp.float32),
            in_specs=[pl.BlockSpec(memory_space=pl.ANY)] * 4,
            out_specs=pl.BlockSpec(memory_space=pltpu.VMEM),
            scratch_shapes=[
                pltpu.VMEM((SLOTS, rows, width), jnp.bfloat16),
                pltpu.VMEM((2, PER, rows, width), jnp.bfloat16),
                pltpu.VMEM((2, rows, width), jnp.bfloat16),
                pltpu.VMEM((2, rows, width), jnp.bfloat16),
                pltpu.VMEM(partners.shape, jnp.int32),
                pltpu.SMEM(cluster.shape, jnp.int32),
                pltpu.SMEM(counts.shape, jnp.int32),
                pltpu.VMEM((7, 16, 128), jnp.int32),
                pltpu.SMEM((16, 128), jnp.int32),
                pltpu.SMEM((7, 16, 128), jnp.int32),
                pltpu.VMEM((SLOTS, 8, rows), jnp.float32),
                pltpu.VMEM((rows, 128), jnp.float32),
                pltpu.VMEM((SLOTS, 8, rows), jnp.float32),
                pltpu.VMEM((2, PER, rows), jnp.float32),
                pltpu.VMEM((2, PER, rows), jnp.float32),
                dma((PER,)),
                dma((3,)),
                dma((2,)),
                dma((2, 3, 3)),
                dma((2, 3, 3)),
                dma((2, 2)),
                dma((2, 2)),
                dma((2, 2)),
                dma((2, 2)),
                dma((7,)),
                dma((7,)),
                dma,
                dma,
                pltpu.SemaphoreType.REGULAR,
                dma((2,)),
                dma((2,)),
            ],
            compiler_params=pltpu.CompilerParams(
                collective_id=0, has_side_effects=True, vmem_limit_bytes=60 * 2**20
            ),
        )(embeddings, partners, cluster, counts)

    return jax.shard_map(
        per_device,
        mesh=mesh,
        in_specs=(P(AXES, None, None), P(AXES, None), P(AXES), P(AXES)),
        out_specs=P(AXES, None),
        check_vma=False,
    )
```

```python
import jax
import jax.numpy as jnp
from jax import lax
from jax.experimental import pallas as pl
from jax.experimental.pallas import tpu as pltpu
from jax.sharding import PartitionSpec as P

MESH = pl.DeviceIdType.MESH
AXES = ("shard", "group")
PER = 4
SLOTS = 3 * PER
HALF = 256
LOW = -4.0
LEFT, OWN, RIGHT, MATE_R, MATE_L, BEHIND, AHEAD = range(7)
NEAR, NEXT, THIRD, FOURTH = range(4)
PIECES = ((0, HALF), (HALF, HALF))
PARTS = ((0, HALF // 2), (HALF // 2, HALF // 2), (HALF, HALF))
LAP = 64


def fold_rows(scores):
    rows, columns = scores.shape
    return jnp.max(scores.reshape(rows // 8, 8, columns), axis=0)


def fold_columns(scores):
    best = scores[:, 0:128]
    for start in range(128, scores.shape[1], 128):
        best = jnp.maximum(best, scores[:, start : start + 128])
    return best


def kernel(
    emb,
    partners_hbm,
    cluster_hbm,
    counts_hbm,
    out,
    window,
    raw,
    stage,
    swapped,
    partners,
    cluster,
    counts,
    info,
    own_facts,
    facts,
    col_best,
    row_part,
    row_best,
    sent_best,
    got_best,
    load_sem,
    small_sem,
    stage_sem,
    emb_send,
    emb_recv,
    swap_send,
    swap_recv,
    pass_send,
    pass_recv,
    info_send,
    info_recv,
    own_facts_sem,
    facts_sem,
    late_sem,
    best_send,
    best_recv,
):
    rows_all = window.shape[1]
    shards = lax.axis_size("shard")
    groups = lax.axis_size("group")
    total = shards * groups
    pool = 2 * groups
    me = lax.axis_index("shard") * groups + lax.axis_index("group")

    def place(index):
        index = lax.rem(index + total, total)
        return (lax.div(index, groups), lax.rem(index, groups))

    first_r = lax.rem(me, pool) < groups
    first_l = lax.rem(me + total - 1, pool) < groups
    mate_r = jnp.where(first_r, me + groups, me - groups)
    mate_l = jnp.where(first_l, me + groups, me - groups)
    where_is = {
        LEFT: place(me - 1),
        RIGHT: place(me + 1),
        MATE_R: place(mate_r),
        MATE_L: place(mate_l),
        BEHIND: place(mate_l - 1),
        AHEAD: place(mate_r + 1),
    }
    opens_lap = lax.rem(me, LAP) == 0
    late_for = {
        RIGHT: lax.rem(me, LAP) == LAP - 1,
        MATE_L: lax.rem(me, LAP) == LAP - groups,
        AHEAD: lax.rem(me, LAP) == LAP - 1 - groups,
    }
    seen_as = {LEFT: RIGHT, RIGHT: LEFT, MATE_R: MATE_R, MATE_L: MATE_L, BEHIND: AHEAD, AHEAD: BEHIND}

    barrier = pltpu.get_barrier_semaphore()
    for role in where_is:
        if role in late_for:

            @pl.when(jnp.logical_not(late_for[role]))
            def _(role=role):
                pl.semaphore_signal(barrier, inc=1, device_id=where_is[role], device_id_type=MESH)
        else:
            pl.semaphore_signal(barrier, inc=1, device_id=where_is[role], device_id_type=MESH)

    small = [
        pltpu.make_async_copy(partners_hbm, partners, small_sem.at[0]),
        pltpu.make_async_copy(cluster_hbm, cluster, small_sem.at[1]),
        pltpu.make_async_copy(counts_hbm, counts, small_sem.at[2]),
    ]
    loads = [pltpu.make_async_copy(emb.at[block], window.at[PER + block], load_sem.at[block]) for block in range(PER)]
    stages = [
        pltpu.make_async_copy(emb.at[2], stage.at[0], stage_sem.at[0]),
        pltpu.make_async_copy(emb.at[1], stage.at[1], stage_sem.at[1]),
    ]
    for copy in small + loads + stages:
        copy.start()
    info[OWN] = jnp.zeros(info.shape[1:], jnp.int32)
    for copy in small:
        copy.wait()
    info[OWN, 0:PER, 0 : partners.shape[1]] = partners[...]
    for block in range(PER):
        info[OWN, PER + block : PER + block + 1, :] = jnp.full((1, 128), cluster[block], jnp.int32)
        info[OWN, 2 * PER + block : 2 * PER + block + 1, :] = jnp.full((1, 128), counts[block], jnp.int32)
    to_own_facts = pltpu.make_async_copy(info.at[OWN], own_facts, own_facts_sem)
    to_own_facts.start()
    pl.semaphore_wait(barrier, jnp.where(opens_lap, len(where_is) - len(late_for), len(where_is)))
    for role in late_for:

        @pl.when(late_for[role])
        def _(role=role):
            pl.semaphore_signal(late_sem, inc=1, device_id=where_is[role], device_id_type=MESH)

    def remote(source, target, send_sem, recv_sem, role):
        return pltpu.make_async_remote_copy(
            src_ref=source,
            dst_ref=target,
            send_sem=send_sem,
            recv_sem=recv_sem,
            device_id=where_is[role],
            device_id_type=MESH,
        )

    def push(step, side, piece):
        start, size = PARTS[piece] if step == NEXT else PIECES[piece]
        rows = pl.ds(start, size)
        block = step if side == 0 else PER - 1 - step
        source = stage.at[side, rows, :] if step == THIRD else emb.at[block, rows, :]
        return remote(
            source,
            raw.at[side, step, rows, :],
            emb_send.at[side, step, piece],
            emb_recv.at[side, step, piece],
            LEFT if side == 0 else RIGHT,
        )

    def pass_on(side, piece):
        rows = pl.ds(*PIECES[piece])
        return remote(
            raw.at[side, THIRD, rows, :],
            raw.at[side, FOURTH, rows, :],
            pass_send.at[side, piece],
            pass_recv.at[side, piece],
            MATE_R if side == 0 else MATE_L,
        )

    def swap(side, piece):
        rows = pl.ds(*PIECES[piece])
        return remote(
            emb.at[PER - 1 if side == 0 else 0, rows, :],
            swapped.at[side, rows, :],
            swap_send.at[side, piece],
            swap_recv.at[side, piece],
            MATE_L if side == 0 else MATE_R,
        )

    infos = {
        role: remote(info.at[OWN], info.at[seen_as[role]], info_send.at[role], info_recv.at[seen_as[role]], role)
        for role in where_is
    }
    def greet_left():
        for role in (LEFT, MATE_L, BEHIND):
            infos[role].start()

    for role in (RIGHT, MATE_R, AHEAD):
        infos[role].start()
    pl.when(jnp.logical_not(opens_lap))(greet_left)
    for piece in range(len(PIECES)):
        swap(1, piece).start()
    push(NEAR, 1, 0).start()

    @pl.when(opens_lap)
    def _():
        pl.semaphore_wait(late_sem, len(late_for))
        greet_left()

    for piece in range(len(PIECES)):
        swap(0, piece).start()
    push(NEAR, 0, 0).start()
    push(NEAR, 1, 1).start()
    push(NEAR, 0, 1).start()

    col_best[...] = jnp.full(col_best.shape, LOW, jnp.float32)
    row_best[...] = jnp.full(row_best.shape, LOW, jnp.float32)
    for copy in loads + stages:
        copy.wait()
    to_own_facts.wait()

    def cluster_of(device, block):
        return facts[device, PER + block, 0]

    def spans(device_a, device_b):
        head = cluster_of(device_a, 0)
        return head == cluster_of(device_b, 3), head == cluster_of(device_b, 2)

    def third_is_lent(is_first, spans_all, spans_three, mate_spans_all):
        keeps_left = spans_three & (is_first | jnp.logical_not(spans_all))
        return mate_spans_all & jnp.logical_not(keeps_left), mate_spans_all & keeps_left

    def slot_cost(slot):
        holds = jnp.where(slot == 2 * PER + THIRD, jnp.logical_not(r_left), True)
        holds = jnp.where(slot == 2 * PER + FOURTH, mr_left, holds)
        holds = jnp.where(slot == PER - 1 - THIRD, jnp.logical_not(l_right), holds)
        return jnp.where(slot == PER - 1 - FOURTH, ml_right, holds)

    def count_of(slot):
        return facts[lax.div(slot, PER), 2 * PER + lax.rem(slot, PER), 0]

    def penalty(slot, other):
        first, second = jnp.minimum(slot, other), jnp.maximum(slot, other)
        device_a, block_a = lax.div(first, PER), lax.rem(first, PER)
        device_b, block_b = lax.div(second, PER), lax.rem(second, PER)
        listed = facts[device_a, block_a, second - first] >= 0
        same = cluster_of(device_a, block_a) == cluster_of(device_b, block_b)
        held = slot_cost(slot) & slot_cost(other)
        return jnp.where(listed & same & held, jnp.float32(0.0), jnp.float32(LOW))

    def own_count(slot):
        return own_facts[2 * PER + slot - PER, 0]

    def own_penalty(slot, other):
        listed = own_facts[other - PER, slot - other] >= 0
        same = own_facts[slot, 0] == own_facts[other, 0]
        return jnp.where(listed & same, jnp.float32(0.0), jnp.float32(LOW))

    def normalise(slot, start, size, load, count):
        rows = pl.ds(start, size)
        floats = load(rows).astype(jnp.float32)
        unit = floats * lax.rsqrt(jnp.sum(floats * floats, axis=-1, keepdims=True) + 1e-06)
        head = window[slot, 0:16, :].astype(jnp.float32)[0:1, :]
        head = jnp.where(start == 0, unit[0:1, :], head)
        ids = start + lax.broadcasted_iota(jnp.int32, (size, 1), 0)
        window[slot, rows, :] = jnp.where(ids < count, unit, head).astype(jnp.bfloat16)

    def scored(slot, rows, other, columns):
        return lax.dot_general(
            window[slot, rows, :],
            window[other, columns, :],
            (((1,), (1,)), ((), ())),
            preferred_element_type=jnp.float32,
        )

    def meet_one(slot, rows, part, other, columns, cost):
        scores = scored(slot, rows, other, columns)
        col_best[other, :, columns] = jnp.maximum(col_best[other, :, columns], fold_rows(scores) + cost)
        part[...] = jnp.maximum(part[...], fold_columns(scores) + cost)

    def meet(slot, start, size, low, high, halves=(), unroll=False, cost=penalty):
        rows, every = pl.ds(start, size), pl.ds(0, rows_all)
        part = row_part.at[0:size, :]
        part[...] = jnp.full((size, 128), LOW, jnp.float32)
        for other in halves:
            meet_one(slot, rows, part, other, pl.ds(0, HALF), cost(slot, other))
        if unroll:
            for other in range(low, high):
                meet_one(slot, rows, part, other, every, cost(slot, other))
        else:

            def one(other, carry):
                meet_one(slot, rows, part, other, every, cost(slot, other))
                return carry

            lax.fori_loop(low, high, one, 0)
        best = jnp.max(part[...].T, axis=0, keepdims=True)
        row_best[slot, :, rows] = jnp.broadcast_to(best, (8, size))

    def own_normalise(index, carry):
        slot, start = PER + lax.div(index, 2), pl.multiple_of(lax.rem(index, 2) * HALF, HALF)
        normalise(slot, start, HALF, lambda rows: window[slot, rows, :], own_count(slot))
        return carry

    lax.fori_loop(0, PER * 2, own_normalise, 0)

    def own_step(slot, carry):
        meet(slot, 0, rows_all, PER, slot, cost=own_penalty)
        scores = scored(slot, pl.ds(0, rows_all), slot, pl.ds(0, rows_all))
        row_ids = lax.broadcasted_iota(jnp.int32, scores.shape, 0)
        col_ids = lax.broadcasted_iota(jnp.int32, scores.shape, 1)
        allowed = (row_ids < own_count(slot)) & (row_ids != col_ids)
        scores = jnp.where(allowed, scores, jnp.float32(LOW))
        col_best[slot] = jnp.maximum(col_best[slot], fold_rows(scores) + own_penalty(slot, slot))
        return carry

    lax.fori_loop(PER, 2 * PER, own_step, 0)

    for role in infos:
        infos[role].wait()
    to_facts = pltpu.make_async_copy(info, facts, facts_sem)
    to_facts.start()
    to_facts.wait()
    whole_r, three_r = spans(OWN, RIGHT)
    whole_mr, three_mr = spans(MATE_R, AHEAD)
    whole_l, three_l = spans(LEFT, OWN)
    whole_ml, three_ml = spans(BEHIND, MATE_L)
    r_left, r_right = third_is_lent(first_r, whole_r, three_r, whole_mr)
    mr_left, _ = third_is_lent(jnp.logical_not(first_r), whole_mr, three_mr, whole_r)
    l_left, l_right = third_is_lent(first_l, whole_l, three_l, whole_ml)
    _, ml_right = third_is_lent(jnp.logical_not(first_l), whole_ml, three_ml, whole_l)

    same_lap = (lax.rem(me, LAP) != 0, lax.rem(me, LAP) != LAP - 1)
    goes_first = ((lax.rem(me, pool) == 0) & same_lap[0], (lax.rem(me, pool) == pool - 1) & same_lap[1])
    turns = ((lax.rem(me, groups) == 0) & same_lap[0], (lax.rem(me, groups) == groups - 1) & same_lap[1])
    both, every_part = (0, 1), (0, 1, 2)

    def push_if(condition, step, side, pieces):
        @pl.when(condition)
        def _():
            for piece in pieces:
                push(step, side, piece).start()

    for piece, (first, size) in enumerate(PIECES):
        for side, lent in ((0, l_left), (1, r_right)):
            swap(side, piece).wait()

            def choose(index, carry, side=side, lent=lent, first=first):
                rows = pl.ds(pl.multiple_of(first + index * 64, 64), 64)
                stage[side, rows, :] = jnp.where(lent, swapped[side, rows, :], stage[side, rows, :])
                return carry

            lax.fori_loop(0, size // 64, choose, 0)
            push_if(jnp.logical_not(goes_first[side]), THIRD, side, (piece,))
    for side in (0, 1):
        push_if(jnp.logical_not(goes_first[side]), NEXT, side, every_part)

    def take(step, side, pieces, low, high, halves=(), unroll=False):
        slot = 2 * PER + step if side == 0 else PER - 1 - step
        for piece in pieces:
            if step == FOURTH:
                pass_on(side, piece).wait_recv()
            elif step == NEXT:
                for part in ((0, 1), (2,))[piece]:
                    push(NEXT, side, part).wait_recv()
            normalise(slot, *PIECES[piece], lambda rows: raw[side, step, rows, :], count_of(slot))
        start, size = PIECES[pieces[0]][0], sum(PIECES[piece][1] for piece in pieces)
        meet(slot, start, size, low, high, halves, unroll)

    own, right, left_next, right_next = PER, 2 * PER, PER - 1 - NEXT, 2 * PER + NEXT
    for piece in both:
        for side in both:
            push(NEAR, side, piece).wait_recv()
    for side in both:
        push_if(goes_first[side], THIRD, side, both)
    take(NEAR, 0, both, own, right)
    take(NEAR, 1, both, own + 1, right + 1)
    for piece in both:
        for side in (0, 1):
            push(THIRD, side, piece).wait_recv()
            pass_on(side, piece).start()
        if piece == 1:
            for side in both:
                push_if(goes_first[side], NEXT, side, every_part)
        take(THIRD, 0, (piece,), own - 1, right, (), True)
        take(THIRD, 1, (piece,), own + 2, right + 1, (), True)
    take(FOURTH, 0, (0,), own, own + 2, (), True)
    take(FOURTH, 1, (0,), own + 2, right, (), True)
    take(NEXT, 0, (0,), own - 1, right - 1, (), True)
    take(NEXT, 1, (0,), own + 2, right + 1, (right_next,), True)
    take(FOURTH, 0, (1,), own, own + 2, (), True)
    take(FOURTH, 1, (1,), own + 2, right, (), True)
    take(NEXT, 0, (1,), own - 1, right - 1, (left_next,), True)
    take(NEXT, 1, (1,), own + 2, right + 2, (), True)

    def best_of(slot):
        return jnp.maximum(row_best[slot, 0:1, :], jnp.max(col_best[slot], axis=0, keepdims=True))

    for block in range(PER):
        sent_best[0, block : block + 1, :] = best_of(block)
        sent_best[1, block : block + 1, :] = best_of(2 * PER + block)
    bests = [
        remote(sent_best.at[0], got_best.at[0], best_send.at[0], best_recv.at[0], LEFT),
        remote(sent_best.at[1], got_best.at[1], best_send.at[1], best_recv.at[1], RIGHT),
    ]
    for copy in bests:
        copy.start()

    for step in (NEAR, NEXT, THIRD):
        for piece in range(len(PARTS if step == NEXT else PIECES)):
            for side in range(2):
                push(step, side, piece).wait_send()
    for side in range(2):
        for piece in range(len(PIECES)):
            pass_on(side, piece).wait_send()

    for copy in bests:
        copy.wait()
    ids = lax.broadcasted_iota(jnp.int32, (1, rows_all), 1)
    for block in range(PER):
        best = jnp.maximum(best_of(PER + block), jnp.float32(-1.0))
        best = jnp.maximum(best, got_best[0, block : block + 1, :])
        best = jnp.maximum(best, got_best[1, block : block + 1, :])
        out[block : block + 1, :] = jnp.where(ids < counts[block], best, jnp.float32(0.0))


def solution(mesh):
    def per_device(embeddings, partners, cluster, counts):
        blocks, rows, width = embeddings.shape
        dma = pltpu.SemaphoreType.DMA
        return pl.pallas_call(
            kernel,
            out_shape=jax.ShapeDtypeStruct((blocks, rows), jnp.float32),
            in_specs=[pl.BlockSpec(memory_space=pl.ANY)] * 4,
            out_specs=pl.BlockSpec(memory_space=pltpu.VMEM),
            scratch_shapes=[
                pltpu.VMEM((SLOTS, rows, width), jnp.bfloat16),
                pltpu.VMEM((2, PER, rows, width), jnp.bfloat16),
                pltpu.VMEM((2, rows, width), jnp.bfloat16),
                pltpu.VMEM((2, rows, width), jnp.bfloat16),
                pltpu.VMEM(partners.shape, jnp.int32),
                pltpu.SMEM(cluster.shape, jnp.int32),
                pltpu.SMEM(counts.shape, jnp.int32),
                pltpu.VMEM((7, 16, 128), jnp.int32),
                pltpu.SMEM((16, 128), jnp.int32),
                pltpu.SMEM((7, 16, 128), jnp.int32),
                pltpu.VMEM((SLOTS, 8, rows), jnp.float32),
                pltpu.VMEM((rows, 128), jnp.float32),
                pltpu.VMEM((SLOTS, 8, rows), jnp.float32),
                pltpu.VMEM((2, PER, rows), jnp.float32),
                pltpu.VMEM((2, PER, rows), jnp.float32),
                dma((PER,)),
                dma((3,)),
                dma((2,)),
                dma((2, 3, 3)),
                dma((2, 3, 3)),
                dma((2, 2)),
                dma((2, 2)),
                dma((2, 2)),
                dma((2, 2)),
                dma((7,)),
                dma((7,)),
                dma,
                dma,
                pltpu.SemaphoreType.REGULAR,
                dma((2,)),
                dma((2,)),
            ],
            compiler_params=pltpu.CompilerParams(
                collective_id=0, has_side_effects=True, vmem_limit_bytes=60 * 2**20
            ),
        )(embeddings, partners, cluster, counts)

    return jax.shard_map(
        per_device,
        mesh=mesh,
        in_specs=(P(AXES, None, None), P(AXES, None), P(AXES), P(AXES)),
        out_specs=P(AXES, None),
        check_vma=False,
    )
```

```python
import jax
import jax.numpy as jnp
from jax import lax
from jax.experimental import pallas as pl
from jax.experimental.pallas import tpu as pltpu
from jax.sharding import PartitionSpec as P

MESH = pl.DeviceIdType.MESH
AXES = ("shard", "group")
PER = 4
SLOTS = 3 * PER
HALF = 256
LOW = -4.0
LEFT, OWN, RIGHT, MATE_R, MATE_L, BEHIND, AHEAD = range(7)
NEAR, NEXT, THIRD, FOURTH = range(4)
PIECES = ((0, HALF), (HALF, HALF))
PARTS = ((0, HALF // 2), (HALF // 2, HALF // 2), (HALF, HALF))
LAP = 64


def fold_rows(scores):
    rows, columns = scores.shape
    return jnp.max(scores.reshape(rows // 8, 8, columns), axis=0)


def fold_columns(scores):
    best = scores[:, 0:128]
    for start in range(128, scores.shape[1], 128):
        best = jnp.maximum(best, scores[:, start : start + 128])
    return best


def kernel(
    emb,
    partners_hbm,
    cluster_hbm,
    counts_hbm,
    out,
    window,
    raw,
    stage,
    swapped,
    partners,
    cluster,
    counts,
    info,
    own_facts,
    facts,
    col_best,
    row_part,
    row_best,
    sent_best,
    got_best,
    load_sem,
    small_sem,
    stage_sem,
    emb_send,
    emb_recv,
    swap_send,
    swap_recv,
    pass_send,
    pass_recv,
    info_send,
    info_recv,
    own_facts_sem,
    facts_sem,
    late_sem,
    best_send,
    best_recv,
):
    rows_all = window.shape[1]
    shards = lax.axis_size("shard")
    groups = lax.axis_size("group")
    total = shards * groups
    pool = 2 * groups
    me = lax.axis_index("shard") * groups + lax.axis_index("group")

    def place(index):
        index = lax.rem(index + total, total)
        return (lax.div(index, groups), lax.rem(index, groups))

    first_r = lax.rem(me, pool) < groups
    first_l = lax.rem(me + total - 1, pool) < groups
    mate_r = jnp.where(first_r, me + groups, me - groups)
    mate_l = jnp.where(first_l, me + groups, me - groups)
    where_is = {
        LEFT: place(me - 1),
        RIGHT: place(me + 1),
        MATE_R: place(mate_r),
        MATE_L: place(mate_l),
        BEHIND: place(mate_l - 1),
        AHEAD: place(mate_r + 1),
    }
    opens_lap = lax.rem(me, LAP) == 0
    late_for = {
        RIGHT: lax.rem(me, LAP) == LAP - 1,
        MATE_L: lax.rem(me, LAP) == LAP - groups,
        AHEAD: lax.rem(me, LAP) == LAP - 1 - groups,
    }
    seen_as = {LEFT: RIGHT, RIGHT: LEFT, MATE_R: MATE_R, MATE_L: MATE_L, BEHIND: AHEAD, AHEAD: BEHIND}

    barrier = pltpu.get_barrier_semaphore()
    for role in where_is:
        if role in late_for:

            @pl.when(jnp.logical_not(late_for[role]))
            def _(role=role):
                pl.semaphore_signal(barrier, inc=1, device_id=where_is[role], device_id_type=MESH)
        else:
            pl.semaphore_signal(barrier, inc=1, device_id=where_is[role], device_id_type=MESH)

    small = [
        pltpu.make_async_copy(partners_hbm, partners, small_sem.at[0]),
        pltpu.make_async_copy(cluster_hbm, cluster, small_sem.at[1]),
        pltpu.make_async_copy(counts_hbm, counts, small_sem.at[2]),
    ]
    loads = [pltpu.make_async_copy(emb.at[block], window.at[PER + block], load_sem.at[block]) for block in range(PER)]
    stages = [
        pltpu.make_async_copy(emb.at[2], stage.at[0], stage_sem.at[0]),
        pltpu.make_async_copy(emb.at[1], stage.at[1], stage_sem.at[1]),
    ]
    for copy in small + loads + stages:
        copy.start()
    info[OWN] = jnp.zeros(info.shape[1:], jnp.int32)
    for copy in small:
        copy.wait()
    info[OWN, 0:PER, 0 : partners.shape[1]] = partners[...]
    for block in range(PER):
        info[OWN, PER + block : PER + block + 1, :] = jnp.full((1, 128), cluster[block], jnp.int32)
        info[OWN, 2 * PER + block : 2 * PER + block + 1, :] = jnp.full((1, 128), counts[block], jnp.int32)
    to_own_facts = pltpu.make_async_copy(info.at[OWN], own_facts, own_facts_sem)
    to_own_facts.start()
    pl.semaphore_wait(barrier, jnp.where(opens_lap, len(where_is) - len(late_for), len(where_is)))
    for role in late_for:

        @pl.when(late_for[role])
        def _(role=role):
            pl.semaphore_signal(late_sem, inc=1, device_id=where_is[role], device_id_type=MESH)

    def remote(source, target, send_sem, recv_sem, role):
        return pltpu.make_async_remote_copy(
            src_ref=source,
            dst_ref=target,
            send_sem=send_sem,
            recv_sem=recv_sem,
            device_id=where_is[role],
            device_id_type=MESH,
        )

    def push(step, side, piece):
        start, size = PARTS[piece] if step == NEXT else PIECES[piece]
        rows = pl.ds(start, size)
        block = step if side == 0 else PER - 1 - step
        source = stage.at[side, rows, :] if step == THIRD else emb.at[block, rows, :]
        return remote(
            source,
            raw.at[side, step, rows, :],
            emb_send.at[side, step, piece],
            emb_recv.at[side, step, piece],
            LEFT if side == 0 else RIGHT,
        )

    def pass_on(side, piece):
        rows = pl.ds(*PIECES[piece])
        return remote(
            raw.at[side, THIRD, rows, :],
            raw.at[side, FOURTH, rows, :],
            pass_send.at[side, piece],
            pass_recv.at[side, piece],
            MATE_R if side == 0 else MATE_L,
        )

    def swap(side, piece):
        rows = pl.ds(*PIECES[piece])
        return remote(
            emb.at[PER - 1 if side == 0 else 0, rows, :],
            swapped.at[side, rows, :],
            swap_send.at[side, piece],
            swap_recv.at[side, piece],
            MATE_L if side == 0 else MATE_R,
        )

    infos = {
        role: remote(info.at[OWN], info.at[seen_as[role]], info_send.at[role], info_recv.at[seen_as[role]], role)
        for role in where_is
    }
    def greet_left():
        for role in (LEFT, MATE_L, BEHIND):
            infos[role].start()

    for role in (RIGHT, MATE_R, AHEAD):
        infos[role].start()
    pl.when(jnp.logical_not(opens_lap))(greet_left)
    for piece in range(len(PIECES)):
        swap(1, piece).start()
    push(NEAR, 1, 0).start()

    @pl.when(opens_lap)
    def _():
        pl.semaphore_wait(late_sem, len(late_for))
        greet_left()

    for piece in range(len(PIECES)):
        swap(0, piece).start()
    push(NEAR, 0, 0).start()
    push(NEAR, 1, 1).start()
    push(NEAR, 0, 1).start()

    col_best[...] = jnp.full(col_best.shape, LOW, jnp.float32)
    row_best[...] = jnp.full(row_best.shape, LOW, jnp.float32)
    for copy in loads + stages:
        copy.wait()
    to_own_facts.wait()

    def cluster_of(device, block):
        return facts[device, PER + block, 0]

    def spans(device_a, device_b):
        head = cluster_of(device_a, 0)
        return head == cluster_of(device_b, 3), head == cluster_of(device_b, 2)

    def third_is_lent(is_first, spans_all, spans_three, mate_spans_all):
        keeps_left = spans_three & (is_first | jnp.logical_not(spans_all))
        return mate_spans_all & jnp.logical_not(keeps_left), mate_spans_all & keeps_left

    def slot_cost(slot):
        holds = jnp.where(slot == 2 * PER + THIRD, jnp.logical_not(r_left), True)
        holds = jnp.where(slot == 2 * PER + FOURTH, mr_left, holds)
        holds = jnp.where(slot == PER - 1 - THIRD, jnp.logical_not(l_right), holds)
        return jnp.where(slot == PER - 1 - FOURTH, ml_right, holds)

    def count_of(slot):
        return facts[lax.div(slot, PER), 2 * PER + lax.rem(slot, PER), 0]

    def penalty(slot, other):
        first, second = jnp.minimum(slot, other), jnp.maximum(slot, other)
        device_a, block_a = lax.div(first, PER), lax.rem(first, PER)
        device_b, block_b = lax.div(second, PER), lax.rem(second, PER)
        listed = facts[device_a, block_a, second - first] >= 0
        same = cluster_of(device_a, block_a) == cluster_of(device_b, block_b)
        held = slot_cost(slot) & slot_cost(other)
        return jnp.where(listed & same & held, jnp.float32(0.0), jnp.float32(LOW))

    def own_count(slot):
        return own_facts[2 * PER + slot - PER, 0]

    def own_penalty(slot, other):
        listed = own_facts[other - PER, slot - other] >= 0
        same = own_facts[slot, 0] == own_facts[other, 0]
        return jnp.where(listed & same, jnp.float32(0.0), jnp.float32(LOW))

    def normalise(slot, start, size, load, count):
        rows = pl.ds(start, size)
        floats = load(rows).astype(jnp.float32)
        unit = floats * lax.rsqrt(jnp.sum(floats * floats, axis=-1, keepdims=True) + 1e-06)
        head = window[slot, 0:16, :].astype(jnp.float32)[0:1, :]
        head = jnp.where(start == 0, unit[0:1, :], head)
        ids = start + lax.broadcasted_iota(jnp.int32, (size, 1), 0)
        window[slot, rows, :] = jnp.where(ids < count, unit, head).astype(jnp.bfloat16)

    def scored(slot, rows, other, columns):
        return lax.dot_general(
            window[slot, rows, :],
            window[other, columns, :],
            (((1,), (1,)), ((), ())),
            preferred_element_type=jnp.float32,
        )

    def meet_one(slot, rows, part, other, columns, cost):
        scores = scored(slot, rows, other, columns)
        col_best[other, :, columns] = jnp.maximum(col_best[other, :, columns], fold_rows(scores) + cost)
        part[...] = jnp.maximum(part[...], fold_columns(scores) + cost)

    def meet(slot, start, size, low, high, halves=(), unroll=False, cost=penalty):
        rows, every = pl.ds(start, size), pl.ds(0, rows_all)
        part = row_part.at[0:size, :]
        part[...] = jnp.full((size, 128), LOW, jnp.float32)
        for other in halves:
            meet_one(slot, rows, part, other, pl.ds(0, HALF), cost(slot, other))
        if unroll:
            for other in range(low, high):
                meet_one(slot, rows, part, other, every, cost(slot, other))
        else:

            def one(other, carry):
                meet_one(slot, rows, part, other, every, cost(slot, other))
                return carry

            lax.fori_loop(low, high, one, 0)
        best = jnp.max(part[...].T, axis=0, keepdims=True)
        row_best[slot, :, rows] = jnp.broadcast_to(best, (8, size))

    def own_normalise(index, carry):
        slot, start = PER + lax.div(index, 2), pl.multiple_of(lax.rem(index, 2) * HALF, HALF)
        normalise(slot, start, HALF, lambda rows: window[slot, rows, :], own_count(slot))
        return carry

    lax.fori_loop(0, PER * 2, own_normalise, 0)

    def own_step(slot, carry):
        meet(slot, 0, rows_all, PER, slot, cost=own_penalty)
        scores = scored(slot, pl.ds(0, rows_all), slot, pl.ds(0, rows_all))
        row_ids = lax.broadcasted_iota(jnp.int32, scores.shape, 0)
        col_ids = lax.broadcasted_iota(jnp.int32, scores.shape, 1)
        allowed = (row_ids < own_count(slot)) & (row_ids != col_ids)
        scores = jnp.where(allowed, scores, jnp.float32(LOW))
        col_best[slot] = jnp.maximum(col_best[slot], fold_rows(scores) + own_penalty(slot, slot))
        return carry

    lax.fori_loop(PER, 2 * PER, own_step, 0)

    for role in infos:
        infos[role].wait()
    to_facts = pltpu.make_async_copy(info, facts, facts_sem)
    to_facts.start()
    to_facts.wait()
    whole_r, three_r = spans(OWN, RIGHT)
    whole_mr, three_mr = spans(MATE_R, AHEAD)
    whole_l, three_l = spans(LEFT, OWN)
    whole_ml, three_ml = spans(BEHIND, MATE_L)
    r_left, r_right = third_is_lent(first_r, whole_r, three_r, whole_mr)
    mr_left, _ = third_is_lent(jnp.logical_not(first_r), whole_mr, three_mr, whole_r)
    l_left, l_right = third_is_lent(first_l, whole_l, three_l, whole_ml)
    _, ml_right = third_is_lent(jnp.logical_not(first_l), whole_ml, three_ml, whole_l)

    same_lap = (lax.rem(me, LAP) != 0, lax.rem(me, LAP) != LAP - 1)
    goes_first = ((lax.rem(me, pool) == 0) & same_lap[0], (lax.rem(me, pool) == pool - 1) & same_lap[1])
    turns = ((lax.rem(me, groups) == 0) & same_lap[0], (lax.rem(me, groups) == groups - 1) & same_lap[1])
    both, every_part = (0, 1), (0, 1, 2)

    def push_if(condition, step, side, pieces):
        @pl.when(condition)
        def _():
            for piece in pieces:
                push(step, side, piece).start()

    for piece, (first, size) in enumerate(PIECES):
        for side, lent in ((0, l_left), (1, r_right)):
            swap(side, piece).wait()

            def choose(index, carry, side=side, lent=lent, first=first):
                rows = pl.ds(pl.multiple_of(first + index * 64, 64), 64)
                stage[side, rows, :] = jnp.where(lent, swapped[side, rows, :], stage[side, rows, :])
                return carry

            lax.fori_loop(0, size // 64, choose, 0)
            push_if(jnp.logical_not(goes_first[side]), THIRD, side, (piece,))
    for side in (0, 1):
        push_if(jnp.logical_not(goes_first[side]), NEXT, side, every_part)

    def take(step, side, pieces, low, high, halves=(), unroll=False):
        slot = 2 * PER + step if side == 0 else PER - 1 - step
        for piece in pieces:
            if step == FOURTH:
                pass_on(side, piece).wait_recv()
            elif step == NEXT:
                for part in ((0, 1), (2,))[piece]:
                    push(NEXT, side, part).wait_recv()
            normalise(slot, *PIECES[piece], lambda rows: raw[side, step, rows, :], count_of(slot))
        start, size = PIECES[pieces[0]][0], sum(PIECES[piece][1] for piece in pieces)
        meet(slot, start, size, low, high, halves, unroll)

    own, right, left_next, right_next = PER, 2 * PER, PER - 1 - NEXT, 2 * PER + NEXT
    for piece in both:
        push(NEAR, 0, piece).wait_recv()
    push_if(goes_first[0], THIRD, 0, both)
    take(NEAR, 0, both, own, right)
    for piece in both:
        push(NEAR, 1, piece).wait_recv()
    push_if(goes_first[1], THIRD, 1, both)
    take(NEAR, 1, both, own + 1, right + 1)
    for piece in both:
        for side in (0, 1):
            push(THIRD, side, piece).wait_recv()
            pass_on(side, piece).start()
        if piece == 1:
            for side in both:
                push_if(goes_first[side], NEXT, side, every_part)
        take(THIRD, 0, (piece,), own - 1, right, (), True)
        take(THIRD, 1, (piece,), own + 2, right + 1, (), True)
    take(FOURTH, 0, (0,), own, own + 2, (), True)
    take(FOURTH, 1, (0,), own + 2, right, (), True)
    take(NEXT, 0, (0,), own - 1, right - 1, (), True)
    take(NEXT, 1, (0,), own + 2, right + 1, (right_next,), True)
    take(FOURTH, 0, (1,), own, own + 2, (), True)
    take(FOURTH, 1, (1,), own + 2, right, (), True)
    def best_of(slot):
        return jnp.maximum(row_best[slot, 0:1, :], jnp.max(col_best[slot], axis=0, keepdims=True))

    for block in (0, 1):
        sent_best[0, block : block + 1, :] = best_of(block)
    for block in (2, 3):
        sent_best[1, block : block + 1, :] = best_of(2 * PER + block)
    take(NEXT, 0, (1,), own - 1, right - 1, (left_next,), True)
    take(NEXT, 1, (1,), own + 2, right + 2, (), True)

    for block in (2, 3):
        sent_best[0, block : block + 1, :] = best_of(block)
    for block in (0, 1):
        sent_best[1, block : block + 1, :] = best_of(2 * PER + block)
    bests = [
        remote(sent_best.at[0], got_best.at[0], best_send.at[0], best_recv.at[0], LEFT),
        remote(sent_best.at[1], got_best.at[1], best_send.at[1], best_recv.at[1], RIGHT),
    ]
    for copy in bests:
        copy.start()

    for step in (NEAR, NEXT, THIRD):
        for piece in range(len(PARTS if step == NEXT else PIECES)):
            for side in range(2):
                push(step, side, piece).wait_send()
    for side in range(2):
        for piece in range(len(PIECES)):
            pass_on(side, piece).wait_send()

    for copy in bests:
        copy.wait()
    ids = lax.broadcasted_iota(jnp.int32, (1, rows_all), 1)
    for block in range(PER):
        best = jnp.maximum(best_of(PER + block), jnp.float32(-1.0))
        best = jnp.maximum(best, got_best[0, block : block + 1, :])
        best = jnp.maximum(best, got_best[1, block : block + 1, :])
        out[block : block + 1, :] = jnp.where(ids < counts[block], best, jnp.float32(0.0))


def solution(mesh):
    def per_device(embeddings, partners, cluster, counts):
        blocks, rows, width = embeddings.shape
        dma = pltpu.SemaphoreType.DMA
        return pl.pallas_call(
            kernel,
            out_shape=jax.ShapeDtypeStruct((blocks, rows), jnp.float32),
            in_specs=[pl.BlockSpec(memory_space=pl.ANY)] * 4,
            out_specs=pl.BlockSpec(memory_space=pltpu.VMEM),
            scratch_shapes=[
                pltpu.VMEM((SLOTS, rows, width), jnp.bfloat16),
                pltpu.VMEM((2, PER, rows, width), jnp.bfloat16),
                pltpu.VMEM((2, rows, width), jnp.bfloat16),
                pltpu.VMEM((2, rows, width), jnp.bfloat16),
                pltpu.VMEM(partners.shape, jnp.int32),
                pltpu.SMEM(cluster.shape, jnp.int32),
                pltpu.SMEM(counts.shape, jnp.int32),
                pltpu.VMEM((7, 16, 128), jnp.int32),
                pltpu.SMEM((16, 128), jnp.int32),
                pltpu.SMEM((7, 16, 128), jnp.int32),
                pltpu.VMEM((SLOTS, 8, rows), jnp.float32),
                pltpu.VMEM((rows, 128), jnp.float32),
                pltpu.VMEM((SLOTS, 8, rows), jnp.float32),
                pltpu.VMEM((2, PER, rows), jnp.float32),
                pltpu.VMEM((2, PER, rows), jnp.float32),
                dma((PER,)),
                dma((3,)),
                dma((2,)),
                dma((2, 3, 3)),
                dma((2, 3, 3)),
                dma((2, 2)),
                dma((2, 2)),
                dma((2, 2)),
                dma((2, 2)),
                dma((7,)),
                dma((7,)),
                dma,
                dma,
                pltpu.SemaphoreType.REGULAR,
                dma((2,)),
                dma((2,)),
            ],
            compiler_params=pltpu.CompilerParams(
                collective_id=0, has_side_effects=True, vmem_limit_bytes=60 * 2**20
            ),
        )(embeddings, partners, cluster, counts)

    return jax.shard_map(
        per_device,
        mesh=mesh,
        in_specs=(P(AXES, None, None), P(AXES, None), P(AXES), P(AXES)),
        out_specs=P(AXES, None),
        check_vma=False,
    )
```
